256 devices in a mesh: rep: 8 (over z_hi, core), seq: 16 (over y, x), chip: 2 (over z_lo).
Axes of the slice: x: 4, y: 4, z: 8 (z_hi: 4, z_lo: 2; z = z_hi * 2 + z_lo), core: 2. Of those that a mesh axis runs over, the one named last changes fastest.
Arguments:
- text_rows: bfloat16 [2048, 3072], P('rep', 'seq'), may hold values from -60 to 60
- modulation: float32 [50, 2, 3072], P(None, None, 'seq'), may hold values from -3 to 3
- timestep: int32 [8], replicated, may hold values from 0 to 49
- row_request: int32 [2048, 1], P('rep'), may hold values from 0 to 7; in each aligned block of 16 rows (0 to 15, 16 to 31, ...) at most 4 rows name the same one
- w_key: bfloat16 [3072, 3072], P('seq', 'chip'), may hold values from -0.109375 to 0.109375
- w_value: bfloat16 [3072, 3072], P('seq', 'chip'), may hold values from -0.4375 to 0.4375
- q_image: bfloat16 [8, 1792, 3072], P('rep', ('seq', 'chip')), may hold values from -56 to 56
- k_image: bfloat16 [8, 1792, 3072], P('rep', ('seq', 'chip')), may hold values from -16 to 16
- v_image: bfloat16 [8, 1792, 3072], P('rep', ('seq', 'chip')), may hold values from -24 to 24
Outputs:
- attended: bfloat16 [8, 1792, 3072], P('rep', ('seq', 'chip'))
The draws below stay inside these ranges and needn't reach their ends.
Inputs may be any that keep to these rules, and one draw needn't show every extreme that they name: `row_request`: in each aligned block of 16 rows no request is named by more than 4 rows; every request is named by some row.
All inputs are finite; a program needn't handle non-finite values.
Results may differ from the reference program's by a relative error of at most 0.025.
Values may be sent and summed in bfloat16 or wider, within the bound.
A program may use at most 128 MiB of HBM per device.

```python
import math
import jax
import jax.numpy as jnp
import numpy as np
from jax import lax

D = 3072
HEADS = 24
HEAD_DIM = 128
TXT_DEV = 16
STEPS = 50
CAP = 4
REQS = 8
IMG = 1792
TXT = 2048
LSLOT = 512


def key_field(key):
    return jnp.clip(jax.random.normal(jax.random.fold_in(key, 101), (REQS, IMG, D), jnp.float32), -5.0, 5.0)


def shared_direction(key):
    return jax.random.rademacher(jax.random.fold_in(key, 103), (REQS, 1, D), jnp.float32)


def draw_text_rows(key, part):
    key = jax.random.fold_in(key, 7)
    first, second = jax.random.split(key, 2)
    row_scale = 10.0 ** jax.random.uniform(first, (TXT, 1), jnp.float32)
    column_scale = 10.0 ** (jnp.arange(D, dtype=jnp.float32) / D)
    noise = jnp.clip(jax.random.normal(second, (TXT, D), jnp.float32), -5.0, 5.0)
    return (0.1 * noise * row_scale * column_scale[None, :]).astype(jnp.bfloat16)


def draw_k_image(key, part):
    base = key_field(key)
    common = shared_direction(key)
    key = jax.random.fold_in(key, 3)
    first, second = jax.random.split(key, 2)
    chosen = jax.random.bernoulli(first, 0.3, (REQS, IMG, 1))
    level = jax.random.uniform(second, (REQS, IMG, 1), jnp.float32, 0.4, 0.6)
    aligned = level * common + 0.25 * base
    return jnp.where(chosen, aligned, base).astype(jnp.bfloat16)


def draw_q_image(key, part):
    common = shared_direction(key)
    key = jax.random.fold_in(key, 5)
    field = 2.0 * jnp.clip(jax.random.normal(key, (REQS, IMG, D), jnp.float32), -5.0, 5.0) + 0.35 * common
    return field.astype(jnp.bfloat16)


def set_ends(drawn, own_key, least, largest):
    place = [jax.random.randint(jax.random.fold_in(own_key, axis), (), 0, length) for axis, length in enumerate(drawn.shape)]
    widest = drawn.shape.index(max(drawn.shape))
    beside = place[:widest] + [(place[widest] + 1) % drawn.shape[widest]] + place[widest + 1:]
    return drawn.at[tuple(place)].set(least).at[tuple(beside)].set(largest)


def block_levels(rng, dims, shards, smallest, largest):
    def one(position, parts):
        heights = jax.random.uniform(jax.random.fold_in(jax.random.fold_in(rng, 6), position), (parts,), jnp.float32, smallest / len(shards), largest / len(shards))
        return jnp.repeat(jnp.exp(heights), dims[position] // parts).reshape((-1,) + (1,) * (len(dims) - position - 1))

    factor_of = one(*shards[0])
    for cut in shards[1:]:
        factor_of = factor_of * one(*cut)
    return factor_of


def routed_block(key, own, number, rows, number_of, top, bound, slope):
    sequence = jax.random.permutation(key, number_of)
    heavy_load, usual = load_shares(number_of, rows * top, bound, slope, True), load_shares(number_of, rows * top, bound, slope, False)
    places = jnp.arange(number_of)

    def named(tallies, offset_by):
        used = int((tallies > 0).sum())
        fixed = max(1, used // 4)
        passed = fixed + (places - fixed + offset_by * (used - fixed)) % max(1, number_of - fixed)
        return jnp.zeros((number_of,), jnp.int32).at[sequence[jnp.where(places < fixed, places, passed)]].set(jnp.asarray(tallies, jnp.int32))

    tallies = jnp.where(number % 4 == 0, named(heavy_load, number // 4), named(usual, number - number // 4 - 1))
    mixed = jax.random.permutation(jax.random.fold_in(own, 3), number_of)
    giver, taker = mixed[0:number_of // 2 * 2:2], mixed[1:number_of // 2 * 2:2]
    margin = jnp.minimum(tallies[giver] - 1, bound - tallies[taker]) // 2
    margin = jnp.where((giver == sequence[0]) | (taker == sequence[0]) | (tallies[taker] == 0), 0, jnp.maximum(margin, 0))
    passed = jax.random.randint(jax.random.fold_in(own, 4), (number_of // 2,), 0, 1 << 20) % (margin + 1)
    tallies = tallies.at[giver].add(-passed).at[taker].add(passed)
    labels = jnp.searchsorted(jnp.cumsum(tallies), jnp.arange(rows * top), side="right").astype(jnp.int32)
    grid = labels.reshape(top, rows).T
    grid = grid[jax.random.permutation(jax.random.fold_in(own, 1), rows)]
    offset_by = jax.random.randint(jax.random.fold_in(own, 2), (rows, 1), 0, top)
    return jnp.take_along_axis(grid, (jnp.arange(top)[None, :] + offset_by) % top, axis=1)


def load_shares(number_of, total, reach, skew, full):
    portions = [(1 << 20) // math.isqrt(standing ** skew) + 1 for standing in range(1, number_of + 1)]
    largest = reach if full else min(reach, max(-(-total // number_of), total * portions[0] // sum(portions)))
    least = 1 if total - largest >= number_of - 1 else 0
    given, surplus = [largest] + [least] * (number_of - 1), total - largest - least * (number_of - 1)
    while surplus > 0:
        free = [i for i in range(1, number_of) if given[i] < largest] or [i for i in range(1, number_of) if given[i] < reach]
        whole, remaining = sum([portions[i] for i in free]), surplus
        for i in free:
            more = min(reach - given[i], max(1, remaining * portions[i] // whole), surplus)
            given[i] = given[i] + more
            surplus = surplus - more
    return np.array(given)


def scatter_about(rng, shape, scale, most, shards=(), held_as=jnp.bfloat16):
    gain = block_levels(rng, shape, shards, -0.22, 0.18) if shards else 1.0
    array = jax.random.normal(rng, shape, jnp.float32) * scale * gain
    return jnp.minimum(jnp.maximum(array, -most), most).astype(held_as)


def setup_inputs(seed: int = 0) -> dict:
    key_list = jax.random.split(jax.random.key(seed), 10)
    text_rows = draw_text_rows(jax.random.fold_in(key_list[9], 71), 0)
    modulation = scatter_about(key_list[1], (STEPS, 2, D), 0.5, 3.0, ((2, 16),), jnp.float32)
    timestep = set_ends(jax.random.randint(key_list[2], (REQS,), 0, STEPS), jax.random.fold_in(key_list[2], 1), 0, STEPS - 1).astype(jnp.int32)
    row_request_keys = jax.random.split(jax.random.fold_in(key_list[3], 1), TXT // TXT_DEV)
    row_request_turns = jax.random.permutation(jax.random.fold_in(key_list[3], 3), TXT // TXT_DEV)
    row_request = jax.vmap(lambda own, number: routed_block(jax.random.fold_in(key_list[3], 2), own, number, TXT_DEV, REQS, 1, CAP, 2))(row_request_keys, row_request_turns).reshape((TXT, 1))
    w_key = scatter_about(key_list[4], (D, D), D ** -0.5, 0.109375, ((0, 16), (1, 2)))
    w_value = scatter_about(key_list[5], (D, D), (D // 16) ** -0.5, 0.4375, ((0, 16), (1, 2)))
    q_image = draw_q_image(jax.random.fold_in(key_list[9], 71), 0)
    k_image = draw_k_image(jax.random.fold_in(key_list[9], 71), 0)
    v_image = scatter_about(key_list[8], (REQS, IMG, D), 4.0, 24.0, ((0, 8), (1, 32)))
    return dict(text_rows=text_rows, modulation=modulation, timestep=timestep, row_request=row_request, w_key=w_key, w_value=w_value, q_image=q_image, k_image=k_image, v_image=v_image)


def attend_group(query, keys, values, is_live):
    queries = query.reshape(-1, HEADS, HEAD_DIM).transpose(1, 0, 2)
    keyed = keys.reshape(-1, HEADS, HEAD_DIM).transpose(1, 0, 2)
    valued = values.reshape(-1, HEADS, HEAD_DIM).transpose(1, 0, 2)

    def one_head(operands):
        head_query, head_keys, head_values = operands
        scores = jnp.dot(head_query, head_keys.T, preferred_element_type=jnp.float32) * (1.0 / math.sqrt(HEAD_DIM))
        scores = jnp.where(is_live[None, :], scores, -jnp.inf)
        weights = jnp.exp(scores - lax.optimization_barrier(jnp.max(scores, axis=1, keepdims=True)))
        mixed = jnp.dot(weights.astype(jnp.bfloat16), head_values, preferred_element_type=jnp.float32)
        return mixed / lax.optimization_barrier(jnp.sum(weights, axis=1, keepdims=True))
    outputs = lax.map(one_head, (queries, keyed, valued))
    return outputs.transpose(1, 0, 2).reshape(query.shape).astype(jnp.bfloat16)

def reference(text_rows, modulation, timestep, row_request, w_key, w_value, q_image, k_image, v_image):
    values_text = text_rows.astype(jnp.float32)
    row_mean = lax.optimization_barrier(jnp.sum(values_text, axis=1)) / D
    row_power = lax.optimization_barrier(jnp.sum(values_text * values_text, axis=1)) / D
    request = row_request[:, 0]
    shifts = modulation[timestep[request]]
    normed = (values_text - row_mean[:, None]) * lax.rsqrt(row_power[:, None] - row_mean[:, None] * row_mean[:, None] + 1e-06)
    shaped = (normed * (1.0 + shifts[:, 1]) + shifts[:, 0]).astype(jnp.bfloat16)
    text_keys = jnp.dot(shaped, w_key, preferred_element_type=jnp.float32).astype(jnp.bfloat16)
    text_values = jnp.dot(shaped, w_value, preferred_element_type=jnp.float32).astype(jnp.bfloat16)
    target = request.astype(jnp.int32)
    order = jnp.argsort(target, stable=True)
    groups = jnp.arange(REQS, dtype=jnp.int32)
    counts = lax.optimization_barrier(jnp.sum((target[None, :] == groups[:, None]).astype(jnp.int32), axis=1))
    starts = (jnp.cumsum(counts) - counts).astype(jnp.int32)
    sorted_keys = jnp.concatenate([text_keys[order], jnp.zeros((LSLOT, D), jnp.bfloat16)], axis=0)
    sorted_values = jnp.concatenate([text_values[order], jnp.zeros((LSLOT, D), jnp.bfloat16)], axis=0)

    def one_group(group):
        begin = starts[group]
        slot_keys = lax.dynamic_slice_in_dim(sorted_keys, begin, LSLOT, 0)
        slot_values = lax.dynamic_slice_in_dim(sorted_values, begin, LSLOT, 0)
        is_live = jnp.concatenate([jnp.ones((IMG,), bool), jnp.arange(LSLOT, dtype=jnp.int32) < counts[group]])
        keys = jnp.concatenate([k_image[group], slot_keys], axis=0)
        values = jnp.concatenate([v_image[group], slot_values], axis=0)
        return attend_group(q_image[group], keys, values, is_live)
    return lax.map(one_group, groups)
```

```python
import functools
import math

import jax
import jax.numpy as jnp
from jax import lax
from jax.experimental import pallas as pl
from jax.experimental.pallas import tpu as pltpu
from jax.sharding import PartitionSpec as P

D = 3072
HEAD_DIM = 128
CAP = 4
BLOCK = 16
NX = 4
NY = 4
NZ = 2
REPS = 8
GROUPS = NY * NZ
WIDE = D // GROUPS
HEADS = WIDE // HEAD_DIM
IMG_DEV = 56
CHUNK = GROUPS * IMG_DEV
ROWS = 256
QUARTER = ROWS // NX
SLOTS = QUARTER // BLOCK * CAP
TEXT = REPS * SLOTS
PACKED = 2 * WIDE + 128
FACTOR = math.log2(math.e) / math.sqrt(HEAD_DIM)
LOWEST = -1e30
MESH = pl.DeviceIdType.MESH

S_TEXT, S_MOD, S_WK, S_WV = 0, 4, 8, 12
S_Q, S_K, S_V = 16, 24, 32
S_KX, S_VX, S_STAT, S_SUM = 40, 44, 48, 52
S_REP, S_TX, S_OUT = 56, 64, 68
S_ALL = 76


def kernel(
    text, mod, step, req, w_key, w_value, q_in, k_in, v_in, out,
    tx, md, wk, wv, qb, kvb, stat_s, stat_r, acc, sum_s, sum_r, rep_s, txt, qh, m, l, o, o_s,
    ssem, rsem, lsem,
):
    f32, bf16 = jnp.float32, jnp.bfloat16
    rep, seq, z = lax.axis_index("rep"), lax.axis_index("seq"), lax.axis_index("chip")
    y, x = lax.div(seq, NX), lax.rem(seq, NX)
    gi = z * NY + y

    def group_peer(d):
        t = lax.rem(gi + d, GROUPS)
        return (rep, lax.rem(t, NY) * NX + x, lax.div(t, NY))

    def x_peer(d):
        return (rep, y * NX + lax.rem(x + d, NX), z)

    def y_peer(d):
        return (rep, lax.rem(y + d, NY) * NX + x, z)

    def rep_peer(d):
        return (lax.rem(rep + d, REPS), seq, z)

    def columns(index):
        return pl.ds(pl.multiple_of(index * WIDE, WIDE), WIDE)

    def remote(src, dst, index, peer):
        return pltpu.make_async_remote_copy(
            src_ref=src, dst_ref=dst, send_sem=ssem.at[index], recv_sem=rsem.at[index],
            device_id=peer, device_id_type=MESH,
        )

    barrier = pltpu.get_barrier_semaphore()
    peers = (
        [group_peer(d) for d in range(1, GROUPS)]
        + [x_peer(d) for d in range(1, NX)]
        + [rep_peer(d) for d in range(1, REPS)]
    )
    for peer in peers:
        pl.semaphore_signal(barrier, inc=1, device_id=peer, device_id_type=MESH)

    own = [
        pltpu.make_async_copy(k_in.at[0, :, columns(gi)], kvb.at[0, 0, 0], lsem.at[0]),
        pltpu.make_async_copy(v_in.at[0, :, columns(gi)], kvb.at[0, 1, 0], lsem.at[1]),
        pltpu.make_async_copy(q_in.at[0, :, columns(gi)], qb.at[0], lsem.at[2]),
        pltpu.make_async_copy(w_key.at[:, columns(y)], wk.at[0], lsem.at[3]),
        pltpu.make_async_copy(w_value.at[:, columns(y)], wv.at[0], lsem.at[4]),
    ]
    for copy in own:
        copy.start()
    for g in range(REPS):
        md[0, 2 * g : 2 * g + 2, :] = mod[step[g]]

    pl.semaphore_wait(barrier, len(peers))

    sent = []

    def send(src, dst, index, peer):
        copy = remote(src, dst, index, peer)
        copy.start()
        sent.append(copy)
        return copy

    got_text = [send(text, tx.at[d], S_TEXT + d, y_peer(d)) for d in range(1, NY)]
    got_mod = [send(md.at[0], md.at[d], S_MOD + d, y_peer(d)) for d in range(1, NY)]
    got_k, got_v, got_q, got_w = [], [], [], []
    for d in range(1, GROUPS):
        there = columns(lax.rem(gi + d, GROUPS))
        got_k.append(send(k_in.at[0, :, there], kvb.at[0, 0, d], S_K + d, group_peer(d)))
        got_v.append(send(v_in.at[0, :, there], kvb.at[0, 1, d], S_V + d, group_peer(d)))
    for d in range(1, NY):
        there = columns(lax.rem(y + d, NY))
        got_w.append(send(w_key.at[:, there], wk.at[d], S_WK + d, y_peer(d)))
        got_w.append(send(w_value.at[:, there], wv.at[d], S_WV + d, y_peer(d)))
    for d in range(1, GROUPS):
        there = columns(lax.rem(gi + d, GROUPS))
        got_q.append(send(q_in.at[0, :, there], qb.at[d], S_Q + d, group_peer(d)))

    for copy in got_text:
        copy.wait_recv()

    def text_part(d):
        return (text[...] if d == 0 else tx[d]).astype(f32)

    total, square = None, None
    for d in range(NY):
        part = text_part(d)
        total = part if total is None else total + part
        square = part * part if square is None else square + part * part
    lane = lax.broadcasted_iota(jnp.int32, (ROWS, 128), 1)
    both = jnp.where(
        lane == 0,
        jnp.sum(total, axis=1, keepdims=True),
        jnp.where(lane == 1, jnp.sum(square, axis=1, keepdims=True), 0.0),
    )
    stat_s[...] = both.T[0:8]
    got_stat = [send(stat_s, stat_r.at[d], S_STAT + d, x_peer(d)) for d in range(1, NX)]

    own[0].wait()
    for copy in got_k:
        copy.wait_recv()
    k_right = send(kvb.at[0, 0], kvb.at[1, 0], S_KX + 1, x_peer(1))
    own[1].wait()
    for copy in got_v:
        copy.wait_recv()
    v_left = send(kvb.at[0, 1], kvb.at[3, 1], S_VX + 3, x_peer(3))
    v_right = send(kvb.at[0, 1], kvb.at[1, 1], S_VX + 1, x_peer(1))
    k_left = send(kvb.at[0, 0], kvb.at[3, 0], S_KX + 3, x_peer(3))

    for copy in got_stat:
        copy.wait_recv()
    summed = stat_s[...] + stat_r[1] + stat_r[2] + stat_r[3]
    stats = jnp.concatenate([summed, jnp.zeros((120, ROWS), f32)], axis=0).T
    mean = stats[:, 0:1] / D
    power = stats[:, 1:2] / D
    scaled = lax.rsqrt(power - mean * mean + 1e-06)
    request = req[...]
    lane16 = lax.broadcasted_iota(jnp.int32, (ROWS, 2 * REPS), 1)
    pick_shift = (lane16 == 2 * request).astype(f32)
    pick_scale = (lane16 == 2 * request + 1).astype(f32)
    for copy in got_mod:
        copy.wait_recv()
    for copy in got_w:
        copy.wait_recv()
    own[3].wait()
    own[4].wait()
    for d in range(NY):
        picked = md[d]
        shift = jnp.dot(pick_shift, picked, precision=lax.Precision.HIGHEST, preferred_element_type=f32)
        scale = jnp.dot(pick_scale, picked, precision=lax.Precision.HIGHEST, preferred_element_type=f32)
        shaped = ((text_part(d) - mean) * scaled * (1.0 + scale) + shift).astype(bf16)
        key_part = jnp.dot(shaped, wk[d], preferred_element_type=f32)
        value_part = jnp.dot(shaped, wv[d], preferred_element_type=f32)
        if d == 0:
            acc[:, 0:WIDE] = key_part
            acc[:, WIDE : 2 * WIDE] = value_part
        else:
            acc[:, 0:WIDE] += key_part
            acc[:, WIDE : 2 * WIDE] += value_part
    sum_s[...] = acc[...].astype(bf16)
    got_sum = []
    for d in range(1, NX):
        quarter = pl.ds(pl.multiple_of(lax.rem(x + d, NX) * QUARTER, QUARTER), QUARTER)
        got_sum.append(send(sum_s.at[quarter], sum_r.at[d], S_SUM + d, x_peer(d)))

    quarter = pl.ds(pl.multiple_of(x * QUARTER, QUARTER), QUARTER)
    target = req[quarter, :]
    lane = lax.broadcasted_iota(jnp.int32, (QUARTER, 128), 1)
    is_target = lane == target
    earlier = (
        lax.broadcasted_iota(jnp.int32, (QUARTER, QUARTER), 1)
        < lax.broadcasted_iota(jnp.int32, (QUARTER, QUARTER), 0)
    ).astype(f32).astype(bf16)
    count = jnp.dot(earlier, is_target.astype(f32).astype(bf16), preferred_element_type=f32)
    slot = jnp.sum(jnp.where(is_target, count, 0.0), axis=1, keepdims=True).astype(jnp.int32)
    placing = (lane == target * SLOTS + slot).astype(f32).astype(bf16)

    for copy in got_sum:
        copy.wait_recv()
    rows = acc[quarter, :] + sum_r[1].astype(f32) + sum_r[2].astype(f32) + sum_r[3].astype(f32)
    rows = jnp.concatenate([rows.astype(bf16), jnp.ones((QUARTER, 128), bf16)], axis=1)
    packed = lax.dot_general(placing, rows, (((0,), (0,)), ((), ())), preferred_element_type=f32)
    rep_s[...] = packed.astype(bf16).reshape(REPS, SLOTS, PACKED)
    got_rep = [
        send(rep_s.at[lax.rem(rep + d, REPS)], txt.at[0, d], S_REP + d, rep_peer(d))
        for d in range(1, REPS)
    ]
    txt[0, 0] = rep_s[rep]

    def load_rows(ref, cols):
        block = ref[:, :, cols].astype(f32)
        return block.reshape(CHUNK, HEAD_DIM).astype(bf16)

    def update(h, keys, values, live):
        cols = pl.ds(pl.multiple_of(h * HEAD_DIM, HEAD_DIM), HEAD_DIM)
        s = lax.dot_general(qh[:, cols], keys, (((1,), (1,)), ((), ())), preferred_element_type=f32)
        if live is not None:
            s = jnp.where(live, s, LOWEST)
        before = m[h]
        newest = jnp.maximum(before, jnp.max(s, axis=1, keepdims=True))
        weights = jnp.exp2((s - newest[:, 0:1]) * FACTOR)
        fade = jnp.exp2((before - newest) * FACTOR)
        m[h] = newest
        l[h] = l[h] * fade + jnp.sum(weights, axis=1, keepdims=True)
        o[h] = o[h] * fade + jnp.dot(weights.astype(bf16), values, preferred_element_type=f32)

    def image_chunk(index):
        def one(h, carry):
            cols = pl.ds(pl.multiple_of(h * HEAD_DIM, HEAD_DIM), HEAD_DIM)
            update(h, load_rows(kvb.at[index, 0], cols), load_rows(kvb.at[index, 1], cols), None)
            return carry

        lax.fori_loop(0, HEADS, one, 0)

    m[...] = jnp.full(m.shape, LOWEST, f32)
    l[...] = jnp.zeros(l.shape, f32)
    o[...] = jnp.zeros(o.shape, f32)

    k_right.wait_recv()
    k_far = send(kvb.at[1, 0], kvb.at[2, 0], S_KX + 2, x_peer(1))
    v_left.wait_recv()
    v_far = send(kvb.at[3, 1], kvb.at[2, 1], S_VX + 2, x_peer(3))

    own[2].wait()
    for copy in got_q:
        copy.wait_recv()
    for h in range(HEADS):
        cols = slice(h * HEAD_DIM, (h + 1) * HEAD_DIM)
        qh[:, cols] = load_rows(qb, cols)
    image_chunk(0)

    for copy in got_rep:
        copy.wait_recv()
    got_txt = [send(txt.at[0], txt.at[d], S_TX + d, x_peer(d)) for d in range(1, NX)]

    v_right.wait_recv()
    image_chunk(1)
    k_left.wait_recv()
    image_chunk(3)
    k_far.wait_recv()
    v_far.wait_recv()
    image_chunk(2)
    for copy in got_txt:
        copy.wait_recv()

    flags = txt[:, :, :, 2 * WIDE : PACKED].reshape(NX * TEXT, 128)
    ones = jnp.ones((16, 128), bf16)
    live = lax.dot_general(ones, flags, (((1,), (1,)), ((), ())), preferred_element_type=f32)[0:1] > 0.5

    def text_chunk(h, carry):
        at_k = pl.ds(pl.multiple_of(h * HEAD_DIM, HEAD_DIM), HEAD_DIM)
        at_v = pl.ds(pl.multiple_of((h + HEADS) * HEAD_DIM, HEAD_DIM), HEAD_DIM)
        keys = txt[:, :, :, at_k].reshape(NX * TEXT, HEAD_DIM)
        values = txt[:, :, :, at_v].reshape(NX * TEXT, HEAD_DIM)
        update(h, keys, values, live)
        return carry

    lax.fori_loop(0, HEADS, text_chunk, 0)

    for h in range(HEADS):
        result = (o[h] / l[h]).reshape(GROUPS, IMG_DEV, HEAD_DIM)
        o_s[:, :, h * HEAD_DIM : (h + 1) * HEAD_DIM] = result.astype(bf16)
    for d in range(1, GROUPS):
        send(o_s.at[d], out.at[0, :, columns(gi)], S_OUT + d, group_peer(GROUPS - d))
    last = pltpu.make_async_copy(o_s.at[0], out.at[0, :, columns(gi)], lsem.at[5])
    last.start()
    for d in range(1, GROUPS):
        there = columns(lax.rem(gi + d, GROUPS))
        remote(o_s.at[d], out.at[0, :, there], S_OUT + d, group_peer(d)).wait_recv()
    last.wait()
    for copy in sent:
        copy.wait_send()


def local(text_rows, modulation, timestep, row_request, w_key, w_value, q_image, k_image, v_image):
    f32, bf16 = jnp.float32, jnp.bfloat16
    vmem = pl.BlockSpec(memory_space=pltpu.VMEM)
    smem = pl.BlockSpec(memory_space=pltpu.SMEM)
    hbm = pl.BlockSpec(memory_space=pl.ANY)
    features = text_rows.shape[1]
    return pl.pallas_call(
        kernel,
        out_shape=jax.ShapeDtypeStruct(q_image.shape, bf16),
        in_specs=[vmem, vmem, smem, vmem, hbm, hbm, hbm, hbm, hbm],
        out_specs=hbm,
        scratch_shapes=[
            pltpu.VMEM((NY, ROWS, features), bf16),
            pltpu.VMEM((NY, 2 * REPS, features), f32),
            pltpu.VMEM((NY, features, WIDE), bf16),
            pltpu.VMEM((NY, features, WIDE), bf16),
            pltpu.VMEM((GROUPS, IMG_DEV, WIDE), bf16),
            pltpu.VMEM((NX, 2, GROUPS, IMG_DEV, WIDE), bf16),
            pltpu.VMEM((8, ROWS), f32),
            pltpu.VMEM((NX, 8, ROWS), f32),
            pltpu.VMEM((ROWS, 2 * WIDE), f32),
            pltpu.VMEM((ROWS, 2 * WIDE), bf16),
            pltpu.VMEM((NX, QUARTER, 2 * WIDE), bf16),
            pltpu.VMEM((REPS, SLOTS, PACKED), bf16),
            pltpu.VMEM((NX, REPS, SLOTS, PACKED), bf16),
            pltpu.VMEM((CHUNK, WIDE), bf16),
            pltpu.VMEM((HEADS, CHUNK, HEAD_DIM), f32),
            pltpu.VMEM((HEADS, CHUNK, HEAD_DIM), f32),
            pltpu.VMEM((HEADS, CHUNK, HEAD_DIM), f32),
            pltpu.VMEM((GROUPS, IMG_DEV, WIDE), bf16),
            pltpu.SemaphoreType.DMA((S_ALL,)),
            pltpu.SemaphoreType.DMA((S_ALL,)),
            pltpu.SemaphoreType.DMA((6,)),
        ],
        compiler_params=pltpu.CompilerParams(
            collective_id=0, has_side_effects=True, vmem_limit_bytes=40 * 1024 * 1024
        ),
    )(text_rows, modulation, timestep, row_request, w_key, w_value, q_image, k_image, v_image)


def solution(mesh):
    image = P("rep", ("seq", "chip"), None)
    return jax.shard_map(
        local,
        mesh=mesh,
        in_specs=(
            P("rep", "seq"),
            P(None, None, "seq"),
            P(),
            P("rep", None),
            P("seq", "chip"),
            P("seq", "chip"),
            image,
            image,
            image,
        ),
        out_specs=image,
        check_vma=False,
    )
```

```python
import math

import jax
import jax.numpy as jnp
from jax import lax
from jax.experimental import pallas as pl
from jax.experimental.pallas import tpu as pltpu
from jax.sharding import PartitionSpec as P

D = 3072
HEAD_DIM = 128
CAP = 4
BLOCK = 16
NX = 4
NY = 4
NZ = 2
REPS = 8
PLANE = NX * NY
GROUP = PLANE * NZ
ROLES = 3
WIDE = ROLES * HEAD_DIM
IMG_DEV = 56
IMG = GROUP * IMG_DEV
SLOTS_PER_STEP = 8
STEP = SLOTS_PER_STEP * IMG_DEV
STEPS = GROUP // SLOTS_PER_STEP
ROWS = 256
SLOTS = ROWS // BLOCK * CAP
TEXT = REPS * SLOTS
HALF = 96
FACTOR = math.log2(math.e) / math.sqrt(HEAD_DIM)
LOWEST = -1e30
VMEM_LIMIT = 60 * 1024 * 1024
MESH = pl.DeviceIdType.MESH

S_TEXT, S_MOD, S_STAT, S_REQ = 0, 1, 2, 3
S_W, S_WC, S_SUM, S_REP = 4, 6, 8, 10
S_K, S_Q, S_V, S_OUT = 12, 13, 14, 15
S_ALL = 16


def kernel(
    text, mod, step, req, w_key, w_value, q_in, k_in, v_in, out,
    tx, mod_v, md, rq, w, qb, kb, vb, stats, xs, acc, sum_s, sum_r,
    place_t, rep_s, landed, qh, kh, vh, m, l, o, o_s,
    ssem, rsem, lsem,
):
    f32, bf16 = jnp.float32, jnp.bfloat16
    rep, seq, z = lax.axis_index("rep"), lax.axis_index("seq"), lax.axis_index("chip")
    y, x = lax.div(seq, NX), lax.rem(seq, NX)
    role = lax.rem(x + y, NX)
    active = role < ROLES
    idle = role >= ROLES

    def group_at(px, py, pz):
        return (rep, py * NX + px, pz)

    def ahead(i):
        px = lax.rem(x + lax.rem(i, NX), NX)
        py = lax.rem(y + lax.rem(lax.div(i, NX), NY), NY)
        pz = lax.rem(z + lax.div(i, PLANE), NZ)
        return px, py, pz

    def behind(i):
        px = lax.rem(x + NX - lax.rem(i, NX), NX)
        py = lax.rem(y + NY - lax.rem(lax.div(i, NX), NY), NY)
        pz = lax.rem(z + NZ - lax.div(i, PLANE), NZ)
        return px, py, pz

    def x_peer(d):
        return (rep, y * NX + lax.rem(x + d, NX), z)

    def y_peer(d):
        return (rep, lax.rem(y + d, NY) * NX + x, z)

    def rep_peer(d):
        return (lax.rem(rep + d, REPS), seq, z)

    def head_columns(head):
        return pl.ds(pl.multiple_of(head * HEAD_DIM, HEAD_DIM), HEAD_DIM)

    def columns(index):
        return pl.ds(pl.multiple_of(index * WIDE, WIDE), WIDE)

    own_head = head_columns((z * NY + y) * ROLES + role)

    def remote(src, dst, index, peer):
        return pltpu.make_async_remote_copy(
            src_ref=src, dst_ref=dst, send_sem=ssem.at[index], recv_sem=rsem.at[index],
            device_id=peer, device_id_type=MESH,
        )

    def send(src, dst, index, peer):
        remote(src, dst, index, peer).start()

    def arrived(ref, index):
        remote(ref, ref, index, x_peer(1)).wait_recv()

    def left(ref, index):
        remote(ref, ref, index, x_peer(1)).wait_send()

    barrier = pltpu.get_barrier_semaphore()

    def greet(i, carry):
        pl.semaphore_signal(barrier, inc=1, device_id=group_at(*ahead(i)), device_id_type=MESH)
        return carry

    lax.fori_loop(1, GROUP, greet, 0)
    for d in range(1, REPS):
        pl.semaphore_signal(barrier, inc=1, device_id=rep_peer(d), device_id_type=MESH)

    own = [
        pltpu.make_async_copy(text, tx.at[0], lsem.at[0]),
        pltpu.make_async_copy(mod, mod_v, lsem.at[1]),
        pltpu.make_async_copy(req, rq.at[0], lsem.at[2]),
        pltpu.make_async_copy(w_key.at[:, columns(y)], w.at[0, 0], lsem.at[3]),
        pltpu.make_async_copy(w_value.at[:, columns(y)], w.at[1, 0], lsem.at[4]),
    ]
    own_text, own_mod, own_req, own_wk, own_wv = own
    for copy in own:
        copy.start()
    own_image = [(k_in, kb, 5), (q_in, qb, 6), (v_in, vb, 7)]

    @pl.when(active)
    def _():
        for src, dst, index in own_image:
            pltpu.make_async_copy(src.at[0, :, own_head], dst.at[0], lsem.at[index]).start()

    pl.semaphore_wait(barrier, GROUP - 1 + REPS - 1)

    for d in range(1, NY):
        send(text, tx.at[d], S_TEXT, y_peer(d))

    own_mod.wait()
    for g in range(REPS):
        md[0, 2 * g : 2 * g + 2, :] = mod_v[step[g]]
    for d in range(1, NY):
        send(md.at[0], md.at[d], S_MOD, y_peer(d))

    own_text.wait()
    part = tx[0].astype(f32)
    stats[0] = jnp.concatenate(
        [
            jnp.sum(part, axis=0, keepdims=True),
            jnp.sum(part * part, axis=0, keepdims=True),
            jnp.zeros((6, ROWS), f32),
        ],
        axis=0,
    )

    def send_stats(i, carry):
        send(stats.at[0], stats.at[i], S_STAT, group_at(*ahead(i)))
        return carry

    lax.fori_loop(1, PLANE, send_stats, 0)

    core = lax.rem(rep, 2)
    sibling = (rep + 1 - 2 * core, seq, z)
    half = pl.ds(pl.multiple_of(core * HALF, HALF), HALF)
    for part, src in ((0, w_key), (1, w_value)):
        for d in range(1, NY):
            there = columns(lax.rem(y + d, NY))
            send(src.at[half, there], w.at[part, d, half], S_W + part, y_peer(d))

    def send_image(i, carry):
        px, py, pz = ahead(i)
        its_role = lax.rem(px + py, NX)

        @pl.when(its_role < ROLES)
        def _():
            there = head_columns((pz * NY + py) * ROLES + its_role)
            peer = group_at(px, py, pz)
            send(k_in.at[0, :, there], kb.at[i], S_K, peer)
            send(q_in.at[0, :, there], qb.at[i], S_Q, peer)
            send(v_in.at[0, :, there], vb.at[i], S_V, peer)

        return carry

    lax.fori_loop(1, GROUP, send_image, 0)
    for d in range(1, REPS):
        send(req, rq.at[d], S_REQ, rep_peer(d))

    own_req.wait()
    request = rq[0]
    sub16 = lax.broadcasted_iota(jnp.int32, (16, ROWS), 0)
    is_target = sub16 == request
    first_row = lax.broadcasted_iota(jnp.int32, (ROWS, ROWS), 0)
    second_row = lax.broadcasted_iota(jnp.int32, (ROWS, ROWS), 1)
    earlier = (first_row < second_row).astype(f32).astype(bf16)
    count = jnp.dot(is_target.astype(f32).astype(bf16), earlier, preferred_element_type=f32)
    slot = jnp.sum(jnp.where(is_target, count, 0.0), axis=0, keepdims=True).astype(jnp.int32)
    is_place = lax.broadcasted_iota(jnp.int32, (TEXT, ROWS), 0) == request * SLOTS + slot
    place_t[...] = is_place.astype(f32).astype(bf16)
    pick_shift = (sub16 == 2 * request).astype(f32)
    pick_scale = (sub16 == 2 * request + 1).astype(f32)

    arrived(md.at[1:NY], S_MOD)
    arrived(stats.at[1:PLANE], S_STAT)
    summed = stats[0]
    for i in range(1, PLANE):
        summed = summed + stats[i]
    mean = summed[0:1] / D
    power = summed[1:2] / D
    scaled = lax.rsqrt(power - mean * mean + 1e-06)
    over_rows = (((0,), (0,)), ((), ()))
    arrived(tx.at[1:NY], S_TEXT)
    for d in range(NY):
        shift = lax.dot_general(
            md[d], pick_shift, over_rows, precision=lax.Precision.HIGHEST, preferred_element_type=f32
        )
        scale = lax.dot_general(
            md[d], pick_scale, over_rows, precision=lax.Precision.HIGHEST, preferred_element_type=f32
        )
        shaped = (tx[d].astype(f32) - mean) * scaled * (1.0 + scale) + shift
        xs[d] = shaped.astype(bf16)

    for part in range(2):
        arrived(w.at[part, 1:NY, half], S_W + part)
        send(w.at[part, 1:NY, half], w.at[part, 1:NY, half], S_WC + part, sibling)

    for part, copy in ((0, own_wk), (1, own_wv)):
        copy.wait()
        arrived(w.at[part, 1:NY, half], S_WC + part)
        acc[part] = lax.dot_general(
            xs[...].reshape(D // NX, ROWS), w[part].reshape(D // NX, WIDE), over_rows,
            preferred_element_type=f32,
        )
        sum_s[part] = acc[part].astype(bf16)
        for d in range(1, NX):
            its_role = lax.rem(x + d + y, NX)

            @pl.when(its_role < ROLES)
            def _(part=part, d=d, its_role=its_role):
                src = sum_s.at[part, :, head_columns(its_role)]
                send(src, sum_r.at[part, d], S_SUM + part, x_peer(d))

    @pl.when(active)
    def _():
        for part in range(2):
            arrived(sum_r.at[part, 1:NX], S_SUM + part)
            rows = acc[part, :, head_columns(role)]
            for d in range(1, NX):
                rows = rows + sum_r[part, d].astype(f32)
            moved = jnp.dot(place_t[...], rows.astype(bf16), preferred_element_type=f32)
            rep_s[part] = moved.astype(bf16).reshape(REPS, SLOTS, HEAD_DIM)
            for d in range(1, REPS):
                src = rep_s.at[part, lax.rem(rep + d, REPS)]
                send(src, landed.at[part, d], S_REP + part, rep_peer(d))
            landed[part, 0] = rep_s[part, rep]

        for (src, dst, index), index_all in zip(own_image, (S_K, S_Q, S_V)):
            pltpu.make_async_copy(src.at[0, :, own_head], dst.at[0], lsem.at[index]).wait()
            arrived(dst.at[1:GROUP], index_all)

        def flatten(b, carry):
            slots = pl.ds(b * SLOTS_PER_STEP, SLOTS_PER_STEP)
            rows = pl.ds(pl.multiple_of(b * STEP, STEP), STEP)
            for src, dst in ((kb, kh), (qb, qh), (vb, vh)):
                dst[rows, :] = src[slots].astype(f32).reshape(STEP, HEAD_DIM).astype(bf16)
            return carry

        lax.fori_loop(0, STEPS, flatten, 0)

        over_columns = (((1,), (1,)), ((), ()))

        def image_step(b, carry):
            rows = pl.ds(pl.multiple_of(b * STEP, STEP), STEP)
            s = lax.dot_general(qh[rows, :], kh[...], over_columns, preferred_element_type=f32)
            highest = jnp.max(s, axis=1, keepdims=True)
            weights = jnp.exp2((s - highest) * FACTOR)
            m[rows, :] = jnp.broadcast_to(highest, (STEP, HEAD_DIM))
            l[rows, :] = jnp.broadcast_to(jnp.sum(weights, axis=1, keepdims=True), (STEP, HEAD_DIM))
            o[rows, :] = jnp.dot(weights.astype(bf16), vh[...], preferred_element_type=f32)
            return carry

        lax.fori_loop(0, STEPS, image_step, 0)

        arrived(rq.at[1:REPS], S_REQ)
        named = jnp.concatenate([rq[d] for d in range(REPS)], axis=0) == rep
        counted = jnp.sum(jnp.where(named, 1.0, 0.0), axis=1, keepdims=True)
        lane = lax.broadcasted_iota(jnp.int32, (REPS, TEXT), 1)
        in_rep = lax.broadcasted_iota(jnp.int32, (REPS, TEXT), 0) == lax.div(lane, SLOTS)
        bound = jnp.sum(jnp.where(in_rep, counted, 0.0), axis=0, keepdims=True)
        live = lax.rem(lane, SLOTS)[0:1].astype(f32) < bound

        for part in range(2):
            arrived(landed.at[part, 1:REPS], S_REP + part)

        def text_step(b, carry):
            rows = pl.ds(pl.multiple_of(b * STEP, STEP), STEP)
            keys = landed[0].reshape(TEXT, HEAD_DIM)
            values = landed[1].reshape(TEXT, HEAD_DIM)
            s = lax.dot_general(qh[rows, :], keys, over_columns, preferred_element_type=f32)
            s = jnp.where(live, s, LOWEST)
            before = m[rows, :]
            newest = jnp.maximum(before, jnp.max(s, axis=1, keepdims=True))
            weights = jnp.exp2((s - newest[:, 0:1]) * FACTOR)
            fade = jnp.exp2((before - newest) * FACTOR)
            total = l[rows, :] * fade + jnp.sum(weights, axis=1, keepdims=True)
            mixed = o[rows, :] * fade + jnp.dot(weights.astype(bf16), values, preferred_element_type=f32)
            result = (mixed / total).reshape(SLOTS_PER_STEP, IMG_DEV, HEAD_DIM)
            o_s[pl.ds(b * SLOTS_PER_STEP, SLOTS_PER_STEP)] = result.astype(bf16)

            def send_result(k, inner):
                i = b * SLOTS_PER_STEP + k

                @pl.when(i > 0)
                def _():
                    send(o_s.at[i], out.at[0, :, own_head], S_OUT, group_at(*behind(i)))

                return inner

            lax.fori_loop(0, SLOTS_PER_STEP, send_result, 0)
            return carry

        lax.fori_loop(0, STEPS, text_step, 0)
        last = pltpu.make_async_copy(o_s.at[0], out.at[0, :, own_head], lsem.at[8])
        last.start()
        arrived(out.at[0, :, 0 : (NY * NZ * ROLES - 1) * HEAD_DIM], S_OUT)
        last.wait()
        left(o_s.at[1:GROUP], S_OUT)
        for index in (S_K, S_Q, S_V):
            left(kb.at[1 : NY * NZ * ROLES], index)
        for part in range(2):
            left(sum_r.at[part, 1 : NX - 1], S_SUM + part)
            left(landed.at[part, 1:REPS], S_REP + part)

    @pl.when(idle)
    def _():
        arrived(rq.at[1:REPS], S_REQ)
        arrived(out.at[0], S_OUT)
        for index in (S_K, S_Q, S_V):
            left(kb.at[0 : NY * NZ * ROLES], index)
        for part in range(2):
            left(sum_r.at[part, 1:NX], S_SUM + part)

    left(tx.at[1:NY], S_TEXT)
    left(md.at[1:NY], S_MOD)
    left(stats.at[1:PLANE], S_STAT)
    left(rq.at[1:REPS], S_REQ)
    for part in range(2):
        left(w.at[part, 1:NY, half], S_W + part)
        left(w.at[part, 1:NY, half], S_WC + part)


def local(text_rows, modulation, timestep, row_request, w_key, w_value, q_image, k_image, v_image):
    f32, bf16 = jnp.float32, jnp.bfloat16
    smem = pl.BlockSpec(memory_space=pltpu.SMEM)
    hbm = pl.BlockSpec(memory_space=pl.ANY)
    features = text_rows.shape[1]
    blocks = pltpu.VMEM((GROUP, IMG_DEV, HEAD_DIM), bf16)
    return pl.pallas_call(
        kernel,
        out_shape=jax.ShapeDtypeStruct(q_image.shape, bf16),
        in_specs=[hbm, hbm, smem, hbm, hbm, hbm, hbm, hbm, hbm],
        out_specs=hbm,
        scratch_shapes=[
            pltpu.VMEM((NY, features, ROWS), bf16),
            pltpu.VMEM(modulation.shape, f32),
            pltpu.VMEM((NY, 2 * REPS, features), f32),
            pltpu.VMEM((REPS, 1, ROWS), jnp.int32),
            pltpu.VMEM((2, NY, features, WIDE), bf16),
            blocks,
            blocks,
            blocks,
            pltpu.VMEM((PLANE, 8, ROWS), f32),
            pltpu.VMEM((NY, features, ROWS), bf16),
            pltpu.VMEM((2, ROWS, WIDE), f32),
            pltpu.VMEM((2, ROWS, WIDE), bf16),
            pltpu.VMEM((2, NX, ROWS, HEAD_DIM), bf16),
            pltpu.VMEM((TEXT, ROWS), bf16),
            pltpu.VMEM((2, REPS, SLOTS, HEAD_DIM), bf16),
            pltpu.VMEM((2, REPS, SLOTS, HEAD_DIM), bf16),
            pltpu.VMEM((IMG, HEAD_DIM), bf16),
            pltpu.VMEM((IMG, HEAD_DIM), bf16),
            pltpu.VMEM((IMG, HEAD_DIM), bf16),
            pltpu.VMEM((IMG, HEAD_DIM), f32),
            pltpu.VMEM((IMG, HEAD_DIM), f32),
            pltpu.VMEM((IMG, HEAD_DIM), f32),
            blocks,
            pltpu.SemaphoreType.DMA((S_ALL,)),
            pltpu.SemaphoreType.DMA((S_ALL,)),
            pltpu.SemaphoreType.DMA((9,)),
        ],
        compiler_params=pltpu.CompilerParams(
            collective_id=0, has_side_effects=True, vmem_limit_bytes=VMEM_LIMIT
        ),
    )(
        text_rows.T, modulation, timestep, row_request.reshape(1, -1),
        w_key, w_value, q_image, k_image, v_image,
    )


def solution(mesh):
    image = P("rep", ("seq", "chip"), None)
    return jax.shard_map(
        local,
        mesh=mesh,
        in_specs=(
            P("rep", "seq"),
            P(None, None, "seq"),
            P(),
            P("rep", None),
            P("seq", "chip"),
            P("seq", "chip"),
            image,
            image,
            image,
        ),
        out_specs=image,
        check_vma=False,
    )
```

```python
import math

import jax
import jax.numpy as jnp
from jax import lax
from jax.experimental import pallas as pl
from jax.experimental.pallas import tpu as pltpu
from jax.sharding import PartitionSpec as P

D = 3072
HEAD_DIM = 128
CAP = 4
BLOCK = 16
NX = 4
NY = 4
NZ = 2
REPS = 8
PLANE = NX * NY
GROUP = PLANE * NZ
ROLES = 3
WIDE = ROLES * HEAD_DIM
IMG_DEV = 56
IMG = GROUP * IMG_DEV
SLOTS_PER_STEP = 8
STEP = SLOTS_PER_STEP * IMG_DEV
STEPS = GROUP // SLOTS_PER_STEP
ROWS = 256
SLOTS = ROWS // BLOCK * CAP
TEXT = REPS * SLOTS
HALF = 96
FACTOR = math.log2(math.e) / math.sqrt(HEAD_DIM)
LOWEST = -1e30
VMEM_LIMIT = 60 * 1024 * 1024
MESH = pl.DeviceIdType.MESH

S_TEXT, S_MOD, S_STAT, S_REQ = 0, 1, 2, 3
S_W, S_WC, S_SUM, S_REP = 4, 6, 8, 10
S_OUT, S_HOP, S_LAST = 12, 13, 16
S_ALL = 28


def kernel(
    text, mod, step, req, w_key, w_value, q_in, k_in, v_in, out,
    tx, mod_v, md, rq, w, relay, final, stats, xs, acc, sum_s, sum_r,
    place_t, rep_s, landed, qh, kh, vh, m, l, o, o_s,
    ssem, rsem, lsem,
):
    f32, bf16 = jnp.float32, jnp.bfloat16
    rep, seq, z = lax.axis_index("rep"), lax.axis_index("seq"), lax.axis_index("chip")
    y, x = lax.div(seq, NX), lax.rem(seq, NX)
    role = lax.rem(x + y, NX)
    active = role < ROLES
    idle = role >= ROLES

    def group_at(px, py, pz):
        return (rep, py * NX + px, pz)

    def offsets(i):
        return lax.rem(i, NX), lax.div(i, SLOTS_PER_STEP), lax.rem(lax.div(i, NX), NZ)

    def ahead(i):
        dx, dy, dz = offsets(i)
        return lax.rem(x + dx, NX), lax.rem(y + dy, NY), lax.rem(z + dz, NZ)

    def behind(i):
        dx, dy, dz = offsets(i)
        return lax.rem(x + NX - dx, NX), lax.rem(y + NY - dy, NY), lax.rem(z + NZ - dz, NZ)

    def x_peer(d):
        return (rep, y * NX + lax.rem(x + d, NX), z)

    def y_peer(d):
        return (rep, lax.rem(y + d, NY) * NX + x, z)

    def rep_peer(d):
        return (lax.rem(rep + d, REPS), seq, z)

    def head_columns(head):
        return pl.ds(pl.multiple_of(head * HEAD_DIM, HEAD_DIM), HEAD_DIM)

    def columns(index):
        return pl.ds(pl.multiple_of(index * WIDE, WIDE), WIDE)

    own_head = head_columns((z * NY + y) * ROLES + role)

    def remote(src, dst, index, peer):
        return pltpu.make_async_remote_copy(
            src_ref=src, dst_ref=dst, send_sem=ssem.at[index], recv_sem=rsem.at[index],
            device_id=peer, device_id_type=MESH,
        )

    def send(src, dst, index, peer):
        remote(src, dst, index, peer).start()

    def arrived(ref, index):
        remote(ref, ref, index, x_peer(1)).wait_recv()

    def left(ref, index):
        remote(ref, ref, index, x_peer(1)).wait_send()

    barrier = pltpu.get_barrier_semaphore()

    def greet(i, carry):
        pl.semaphore_signal(barrier, inc=1, device_id=group_at(*ahead(i)), device_id_type=MESH)
        return carry

    lax.fori_loop(1, GROUP, greet, 0)
    for d in range(1, REPS):
        pl.semaphore_signal(barrier, inc=1, device_id=rep_peer(d), device_id_type=MESH)

    own = [
        pltpu.make_async_copy(text, tx.at[0], lsem.at[0]),
        pltpu.make_async_copy(mod, mod_v, lsem.at[1]),
        pltpu.make_async_copy(req, rq.at[0], lsem.at[2]),
        pltpu.make_async_copy(w_key.at[:, columns(y)], w.at[0, 0], lsem.at[3]),
        pltpu.make_async_copy(w_value.at[:, columns(y)], w.at[1, 0], lsem.at[4]),
    ]
    own_text, own_mod, own_req, own_wk, own_wv = own
    for copy in own:
        copy.start()
    def role_at(px, py):
        return lax.rem(px + py, NX)

    def head_at(px, py, pz):
        return head_columns((pz * NY + py) * ROLES + role_at(px, py))

    image = (q_in, k_in, v_in)

    def own_hop(t, d):
        py = lax.rem(y + d, NY)
        return pltpu.make_async_copy(
            image[t].at[0, :, head_at(x, py, z)], relay.at[t, d, 0], lsem.at[5 + NY * t + d]
        )

    for d in range(NY):

        @pl.when(role_at(x, y + d) < ROLES)
        def _(d=d):
            for t in range(3):
                own_hop(t, d).start()

    pl.semaphore_wait(barrier, GROUP - 1 + REPS - 1)

    for d in range(1, NY):
        send(text, tx.at[d], S_TEXT, y_peer(d))

    own_mod.wait()
    for g in range(REPS):
        md[0, 2 * g : 2 * g + 2, :] = mod_v[step[g]]
    for d in range(1, NY):
        send(md.at[0], md.at[d], S_MOD, y_peer(d))

    own_text.wait()
    part = tx[0].astype(f32)
    stats[0] = jnp.concatenate(
        [
            jnp.sum(part, axis=0, keepdims=True),
            jnp.sum(part * part, axis=0, keepdims=True),
            jnp.zeros((6, ROWS), f32),
        ],
        axis=0,
    )

    def send_stats(i, carry):
        px, py = lax.rem(x + lax.rem(i, NX), NX), lax.rem(y + lax.div(i, NX), NY)
        send(stats.at[0], stats.at[i], S_STAT, group_at(px, py, z))
        return carry

    lax.fori_loop(1, PLANE, send_stats, 0)

    core = lax.rem(rep, 2)
    sibling = (rep + 1 - 2 * core, seq, z)
    half = pl.ds(pl.multiple_of(core * HALF, HALF), HALF)
    for part, src in ((0, w_key), (1, w_value)):
        for d in range(1, NY):
            there = columns(lax.rem(y + d, NY))
            send(src.at[half, there], w.at[part, d, half], S_W + part, y_peer(d))

    for t in range(3):

        def first_hop(n, carry, t=t):
            i = lax.rem(n, SLOTS_PER_STEP - 1) + 1
            d = lax.div(n, SLOTS_PER_STEP - 1)
            px, _, pz = ahead(i)
            py = lax.rem(y + d, NY)

            @pl.when(role_at(px, py) < ROLES)
            def _():
                send(image[t].at[0, :, head_at(px, py, pz)], relay.at[t, d, i], S_HOP + t, group_at(px, y, pz))

            return carry

        lax.fori_loop(0, NY * (SLOTS_PER_STEP - 1), first_hop, 0)
    for d in range(1, REPS):
        send(req, rq.at[d], S_REQ, rep_peer(d))

    own_req.wait()
    request = rq[0]
    sub16 = lax.broadcasted_iota(jnp.int32, (16, ROWS), 0)
    is_target = sub16 == request
    first_row = lax.broadcasted_iota(jnp.int32, (ROWS, ROWS), 0)
    second_row = lax.broadcasted_iota(jnp.int32, (ROWS, ROWS), 1)
    earlier = (first_row < second_row).astype(f32).astype(bf16)
    count = jnp.dot(is_target.astype(f32).astype(bf16), earlier, preferred_element_type=f32)
    slot = jnp.sum(jnp.where(is_target, count, 0.0), axis=0, keepdims=True).astype(jnp.int32)
    is_place = lax.broadcasted_iota(jnp.int32, (TEXT, ROWS), 0) == request * SLOTS + slot
    place_t[...] = is_place.astype(f32).astype(bf16)
    pick_shift = (sub16 == 2 * request).astype(f32)
    pick_scale = (sub16 == 2 * request + 1).astype(f32)

    def second_hop(t):
        arrived(relay.at[t, 0:ROLES, 1:SLOTS_PER_STEP], S_HOP + t)
        for d in (1, 3, 2, 0):

            @pl.when(role_at(x, y + d) < ROLES)
            def _(d=d):
                own_hop(t, d).wait()
                if d > 0:
                    send(relay.at[t, d], final.at[t, d], S_LAST + NY * t + d, y_peer(d))

    arrived(md.at[1:NY], S_MOD)
    arrived(stats.at[1:PLANE], S_STAT)
    summed = stats[0]
    for i in range(1, PLANE):
        summed = summed + stats[i]
    mean = summed[0:1] / D
    power = summed[1:2] / D
    scaled = lax.rsqrt(power - mean * mean + 1e-06)
    over_rows = (((0,), (0,)), ((), ()))
    arrived(tx.at[1:NY], S_TEXT)
    for d in range(NY):
        shift = lax.dot_general(
            md[d], pick_shift, over_rows, precision=lax.Precision.HIGHEST, preferred_element_type=f32
        )
        scale = lax.dot_general(
            md[d], pick_scale, over_rows, precision=lax.Precision.HIGHEST, preferred_element_type=f32
        )
        shaped = (tx[d].astype(f32) - mean) * scaled * (1.0 + scale) + shift
        xs[d] = shaped.astype(bf16)

    second_hop(0)
    for part in range(2):
        arrived(w.at[part, 1:NY, half], S_W + part)
        send(w.at[part, 1:NY, half], w.at[part, 1:NY, half], S_WC + part, sibling)

    second_hop(1)
    for part, copy in ((0, own_wk), (1, own_wv)):
        copy.wait()
        arrived(w.at[part, 1:NY, half], S_WC + part)
        acc[part] = lax.dot_general(
            xs[...].reshape(D // NX, ROWS), w[part].reshape(D // NX, WIDE), over_rows,
            preferred_element_type=f32,
        )
        sum_s[part] = acc[part].astype(bf16)
        for d in range(1, NX):
            its_role = lax.rem(x + d + y, NX)

            @pl.when(its_role < ROLES)
            def _(part=part, d=d, its_role=its_role):
                src = sum_s.at[part, :, head_columns(its_role)]
                send(src, sum_r.at[part, d], S_SUM + part, x_peer(d))

    second_hop(2)

    @pl.when(active)
    def _():
        over_columns = (((1,), (1,)), ((), ()))

        def flatten(block):
            return block.astype(f32).reshape(STEP, HEAD_DIM).astype(bf16)

        def image_chunk(c):
            for t, dst in ((1, kh), (2, vh)):
                if c > 0:
                    arrived(final.at[t, c], S_LAST + NY * t + c)
                dst[...] = flatten((final if c > 0 else relay)[t, c])

            def image_step(b, carry):
                rows = pl.ds(pl.multiple_of(b * STEP, STEP), STEP)
                s = lax.dot_general(qh[rows, :], kh[...], over_columns, preferred_element_type=f32)
                highest = jnp.max(s, axis=1, keepdims=True)
                if c == 0:
                    newest = jnp.broadcast_to(highest, (STEP, HEAD_DIM))
                else:
                    newest = jnp.maximum(m[rows, :], highest)
                weights = jnp.exp2((s - newest[:, 0:1]) * FACTOR)
                total = jnp.sum(weights, axis=1, keepdims=True)
                mixed = jnp.dot(weights.astype(bf16), vh[...], preferred_element_type=f32)
                if c == 0:
                    l[rows, :] = jnp.broadcast_to(total, (STEP, HEAD_DIM))
                    o[rows, :] = mixed
                else:
                    fade = jnp.exp2((m[rows, :] - newest) * FACTOR)
                    l[rows, :] = l[rows, :] * fade + total
                    o[rows, :] = o[rows, :] * fade + mixed
                m[rows, :] = newest
                return carry

            lax.fori_loop(0, STEPS, image_step, 0)

        for d in (0, 1, 3, 2):
            if d > 0:
                arrived(final.at[0, d], S_LAST + d)
            qh[pl.ds(d * STEP, STEP), :] = flatten((final if d > 0 else relay)[0, d])
        image_chunk(0)
        image_chunk(1)

        for part in range(2):
            arrived(sum_r.at[part, 1:NX], S_SUM + part)
            rows = acc[part, :, head_columns(role)]
            for d in range(1, NX):
                rows = rows + sum_r[part, d].astype(f32)
            moved = jnp.dot(place_t[...], rows.astype(bf16), preferred_element_type=f32)
            rep_s[part] = moved.astype(bf16).reshape(REPS, SLOTS, HEAD_DIM)
            for d in range(1, REPS):
                src = rep_s.at[part, lax.rem(rep + d, REPS)]
                send(src, landed.at[part, d], S_REP + part, rep_peer(d))
            landed[part, 0] = rep_s[part, rep]

        image_chunk(3)
        image_chunk(2)

        arrived(rq.at[1:REPS], S_REQ)
        named = jnp.concatenate([rq[d] for d in range(REPS)], axis=0) == rep
        counted = jnp.sum(jnp.where(named, 1.0, 0.0), axis=1, keepdims=True)
        lane = lax.broadcasted_iota(jnp.int32, (REPS, TEXT), 1)
        in_rep = lax.broadcasted_iota(jnp.int32, (REPS, TEXT), 0) == lax.div(lane, SLOTS)
        bound = jnp.sum(jnp.where(in_rep, counted, 0.0), axis=0, keepdims=True)
        live = lax.rem(lane, SLOTS)[0:1].astype(f32) < bound

        for part in range(2):
            arrived(landed.at[part, 1:REPS], S_REP + part)

        def text_step(b, carry):
            rows = pl.ds(pl.multiple_of(b * STEP, STEP), STEP)
            keys = landed[0].reshape(TEXT, HEAD_DIM)
            values = landed[1].reshape(TEXT, HEAD_DIM)
            s = lax.dot_general(qh[rows, :], keys, over_columns, preferred_element_type=f32)
            s = jnp.where(live, s, LOWEST)
            before = m[rows, :]
            newest = jnp.maximum(before, jnp.max(s, axis=1, keepdims=True))
            weights = jnp.exp2((s - newest[:, 0:1]) * FACTOR)
            fade = jnp.exp2((before - newest) * FACTOR)
            total = l[rows, :] * fade + jnp.sum(weights, axis=1, keepdims=True)
            mixed = o[rows, :] * fade + jnp.dot(weights.astype(bf16), values, preferred_element_type=f32)
            result = (mixed / total).reshape(SLOTS_PER_STEP, IMG_DEV, HEAD_DIM)
            o_s[pl.ds(b * SLOTS_PER_STEP, SLOTS_PER_STEP)] = result.astype(bf16)

            def send_result(k, inner):
                i = b * SLOTS_PER_STEP + k

                @pl.when(i > 0)
                def _():
                    send(o_s.at[i], out.at[0, :, own_head], S_OUT, group_at(*behind(i)))

                return inner

            lax.fori_loop(0, SLOTS_PER_STEP, send_result, 0)
            return carry

        lax.fori_loop(0, STEPS, text_step, 0)
        last = pltpu.make_async_copy(o_s.at[0], out.at[0, :, own_head], lsem.at[17])
        last.start()
        arrived(out.at[0, :, 0 : (NY * NZ * ROLES - 1) * HEAD_DIM], S_OUT)
        last.wait()
        left(o_s.at[1:GROUP], S_OUT)
        for part in range(2):
            left(sum_r.at[part, 1 : NX - 1], S_SUM + part)
            left(landed.at[part, 1:REPS], S_REP + part)

    @pl.when(idle)
    def _():
        arrived(rq.at[1:REPS], S_REQ)
        arrived(out.at[0], S_OUT)
        for part in range(2):
            left(sum_r.at[part, 1:NX], S_SUM + part)

    for t in range(3):
        left(relay.at[t, 0:ROLES, 1:SLOTS_PER_STEP], S_HOP + t)
        for d in range(1, NY):

            @pl.when(role_at(x, y + d) < ROLES)
            def _(t=t, d=d):
                left(relay.at[t, d], S_LAST + NY * t + d)

    left(tx.at[1:NY], S_TEXT)
    left(md.at[1:NY], S_MOD)
    left(stats.at[1:PLANE], S_STAT)
    left(rq.at[1:REPS], S_REQ)
    for part in range(2):
        left(w.at[part, 1:NY, half], S_W + part)
        left(w.at[part, 1:NY, half], S_WC + part)


def local(text_rows, modulation, timestep, row_request, w_key, w_value, q_image, k_image, v_image):
    f32, bf16 = jnp.float32, jnp.bfloat16
    smem = pl.BlockSpec(memory_space=pltpu.SMEM)
    hbm = pl.BlockSpec(memory_space=pl.ANY)
    features = text_rows.shape[1]
    blocks = pltpu.VMEM((GROUP, IMG_DEV, HEAD_DIM), bf16)
    hops = pltpu.VMEM((3, NY, SLOTS_PER_STEP, IMG_DEV, HEAD_DIM), bf16)
    return pl.pallas_call(
        kernel,
        out_shape=jax.ShapeDtypeStruct(q_image.shape, bf16),
        in_specs=[hbm, hbm, smem, hbm, hbm, hbm, hbm, hbm, hbm],
        out_specs=hbm,
        scratch_shapes=[
            pltpu.VMEM((NY, features, ROWS), bf16),
            pltpu.VMEM(modulation.shape, f32),
            pltpu.VMEM((NY, 2 * REPS, features), f32),
            pltpu.VMEM((REPS, 1, ROWS), jnp.int32),
            pltpu.VMEM((2, NY, features, WIDE), bf16),
            hops,
            hops,
            pltpu.VMEM((PLANE, 8, ROWS), f32),
            pltpu.VMEM((NY, features, ROWS), bf16),
            pltpu.VMEM((2, ROWS, WIDE), f32),
            pltpu.VMEM((2, ROWS, WIDE), bf16),
            pltpu.VMEM((2, NX, ROWS, HEAD_DIM), bf16),
            pltpu.VMEM((TEXT, ROWS), bf16),
            pltpu.VMEM((2, REPS, SLOTS, HEAD_DIM), bf16),
            pltpu.VMEM((2, REPS, SLOTS, HEAD_DIM), bf16),
            pltpu.VMEM((IMG, HEAD_DIM), bf16),
            pltpu.VMEM((STEP, HEAD_DIM), bf16),
            pltpu.VMEM((STEP, HEAD_DIM), bf16),
            pltpu.VMEM((IMG, HEAD_DIM), f32),
            pltpu.VMEM((IMG, HEAD_DIM), f32),
            pltpu.VMEM((IMG, HEAD_DIM), f32),
            blocks,
            pltpu.SemaphoreType.DMA((S_ALL,)),
            pltpu.SemaphoreType.DMA((S_ALL,)),
            pltpu.SemaphoreType.DMA((18,)),
        ],
        compiler_params=pltpu.CompilerParams(
            collective_id=0, has_side_effects=True, vmem_limit_bytes=VMEM_LIMIT
        ),
    )(
        text_rows.T, modulation, timestep, row_request.reshape(1, -1),
        w_key, w_value, q_image, k_image, v_image,
    )


def solution(mesh):
    image = P("rep", ("seq", "chip"), None)
    return jax.shard_map(
        local,
        mesh=mesh,
        in_specs=(
            P("rep", "seq"),
            P(None, None, "seq"),
            P(),
            P("rep", None),
            P("seq", "chip"),
            P("seq", "chip"),
            image,
            image,
            image,
        ),
        out_specs=image,
        check_vma=False,
    )
```

```python
import math

import jax
import jax.numpy as jnp
from jax import lax
from jax.experimental import pallas as pl
from jax.experimental.pallas import tpu as pltpu
from jax.sharding import PartitionSpec as P

D = 3072
HEAD_DIM = 128
CAP = 4
BLOCK = 16
NX = 4
NY = 4
NZ = 2
REPS = 8
PLANE = NX * NY
GROUP = PLANE * NZ
ROLES = 3
WIDE = ROLES * HEAD_DIM
IMG_DEV = 56
IMG = GROUP * IMG_DEV
SLOTS_PER_STEP = 8
STEP = SLOTS_PER_STEP * IMG_DEV
LANES = 896
SLOTS_A_STEP = LANES // IMG_DEV
ROWS = 256
SLOTS = ROWS // BLOCK * CAP
TEXT = REPS * SLOTS
HALF = 96
FACTOR = math.log2(math.e) / math.sqrt(HEAD_DIM)
LOWEST = -1e30
VMEM_LIMIT = 60 * 1024 * 1024
MESH = pl.DeviceIdType.MESH

S_TEXT, S_MOD, S_STAT, S_REQ = 0, 1, 2, 3
S_W, S_WC, S_SUM, S_REP = 4, 6, 8, 10
S_OUT, S_HOP, S_LAST = 12, 13, 16
S_ALL = 28


def kernel(
    text, mod, step, req, w_key, w_value, q_in, k_in, v_in, out,
    tx, mod_v, md, rq, w, relay, final, stats, xs, acc, sum_s, sum_r,
    place_t, rep_s, landed, qh, kh, vh, m, l, o, o_s,
    ssem, rsem, lsem,
):
    f32, bf16 = jnp.float32, jnp.bfloat16
    rep, seq, z = lax.axis_index("rep"), lax.axis_index("seq"), lax.axis_index("chip")
    y, x = lax.div(seq, NX), lax.rem(seq, NX)
    role = lax.rem(x + y, NX)
    active = role < ROLES
    idle = role >= ROLES

    def group_at(px, py, pz):
        return (rep, py * NX + px, pz)

    def offsets(i):
        return lax.rem(i, NX), lax.div(i, SLOTS_PER_STEP), lax.rem(lax.div(i, NX), NZ)

    def ahead(i):
        dx, dy, dz = offsets(i)
        return lax.rem(x + dx, NX), lax.rem(y + dy, NY), lax.rem(z + dz, NZ)

    def behind(i):
        dx, dy, dz = offsets(i)
        return lax.rem(x + NX - dx, NX), lax.rem(y + NY - dy, NY), lax.rem(z + NZ - dz, NZ)

    def x_peer(d):
        return (rep, y * NX + lax.rem(x + d, NX), z)

    def y_peer(d):
        return (rep, lax.rem(y + d, NY) * NX + x, z)

    def rep_peer(d):
        return (lax.rem(rep + d, REPS), seq, z)

    def head_columns(head):
        return pl.ds(pl.multiple_of(head * HEAD_DIM, HEAD_DIM), HEAD_DIM)

    def columns(index):
        return pl.ds(pl.multiple_of(index * WIDE, WIDE), WIDE)

    own_head = head_columns((z * NY + y) * ROLES + role)

    def remote(src, dst, index, peer):
        return pltpu.make_async_remote_copy(
            src_ref=src, dst_ref=dst, send_sem=ssem.at[index], recv_sem=rsem.at[index],
            device_id=peer, device_id_type=MESH,
        )

    def send(src, dst, index, peer):
        remote(src, dst, index, peer).start()

    def arrived(ref, index):
        remote(ref, ref, index, x_peer(1)).wait_recv()

    def left(ref, index):
        remote(ref, ref, index, x_peer(1)).wait_send()

    barrier = pltpu.get_barrier_semaphore()

    def greet(i, carry):
        pl.semaphore_signal(barrier, inc=1, device_id=group_at(*ahead(i)), device_id_type=MESH)
        return carry

    lax.fori_loop(1, GROUP, greet, 0)
    for d in range(1, REPS):
        pl.semaphore_signal(barrier, inc=1, device_id=rep_peer(d), device_id_type=MESH)

    own = [
        pltpu.make_async_copy(text, tx.at[0], lsem.at[0]),
        pltpu.make_async_copy(mod, mod_v, lsem.at[1]),
        pltpu.make_async_copy(req, rq.at[0], lsem.at[2]),
        pltpu.make_async_copy(w_key.at[:, columns(y)], w.at[0, 0], lsem.at[3]),
        pltpu.make_async_copy(w_value.at[:, columns(y)], w.at[1, 0], lsem.at[4]),
    ]
    own_text, own_mod, own_req, own_wk, own_wv = own
    for copy in own:
        copy.start()
    def role_at(px, py):
        return lax.rem(px + py, NX)

    def head_at(px, py, pz):
        return head_columns((pz * NY + py) * ROLES + role_at(px, py))

    image = (q_in, k_in, v_in)

    def own_hop(t, d):
        py = lax.rem(y + d, NY)
        return pltpu.make_async_copy(
            image[t].at[0, :, head_at(x, py, z)], relay.at[t, d, 0], lsem.at[5 + NY * t + d]
        )

    for d in range(NY):

        @pl.when(role_at(x, y + d) < ROLES)
        def _(d=d):
            for t in range(3):
                own_hop(t, d).start()

    pl.semaphore_wait(barrier, GROUP - 1 + REPS - 1)

    for d in range(1, NY):
        send(text, tx.at[d], S_TEXT, y_peer(d))

    own_mod.wait()
    for g in range(REPS):
        md[0, 2 * g : 2 * g + 2, :] = mod_v[step[g]]
    for d in range(1, NY):
        send(md.at[0], md.at[d], S_MOD, y_peer(d))

    own_text.wait()
    part = tx[0].astype(f32)
    stats[0] = jnp.concatenate(
        [
            jnp.sum(part, axis=0, keepdims=True),
            jnp.sum(part * part, axis=0, keepdims=True),
            jnp.zeros((6, ROWS), f32),
        ],
        axis=0,
    )

    def send_stats(i, carry):
        px, py = lax.rem(x + lax.rem(i, NX), NX), lax.rem(y + lax.div(i, NX), NY)
        send(stats.at[0], stats.at[i], S_STAT, group_at(px, py, z))
        return carry

    lax.fori_loop(1, PLANE, send_stats, 0)

    core = lax.rem(rep, 2)
    sibling = (rep + 1 - 2 * core, seq, z)
    half = pl.ds(pl.multiple_of(core * HALF, HALF), HALF)
    for part, src in ((0, w_key), (1, w_value)):
        for d in range(1, NY):
            there = columns(lax.rem(y + d, NY))
            send(src.at[half, there], w.at[part, d, half], S_W + part, y_peer(d))

    for t in range(3):

        def first_hop(n, carry, t=t):
            i = lax.rem(n, SLOTS_PER_STEP - 1) + 1
            d = lax.div(n, SLOTS_PER_STEP - 1)
            px, _, pz = ahead(i)
            py = lax.rem(y + d, NY)

            @pl.when(role_at(px, py) < ROLES)
            def _():
                send(image[t].at[0, :, head_at(px, py, pz)], relay.at[t, d, i], S_HOP + t, group_at(px, y, pz))

            return carry

        lax.fori_loop(0, NY * (SLOTS_PER_STEP - 1), first_hop, 0)
    for d in range(1, REPS):
        send(req, rq.at[d], S_REQ, rep_peer(d))

    own_req.wait()
    request = rq[0]
    sub16 = lax.broadcasted_iota(jnp.int32, (16, ROWS), 0)
    is_target = sub16 == request
    first_row = lax.broadcasted_iota(jnp.int32, (ROWS, ROWS), 0)
    second_row = lax.broadcasted_iota(jnp.int32, (ROWS, ROWS), 1)
    earlier = (first_row < second_row).astype(f32).astype(bf16)
    count = jnp.dot(is_target.astype(f32).astype(bf16), earlier, preferred_element_type=f32)
    slot = jnp.sum(jnp.where(is_target, count, 0.0), axis=0, keepdims=True).astype(jnp.int32)
    is_place = lax.broadcasted_iota(jnp.int32, (TEXT, ROWS), 0) == request * SLOTS + slot
    place_t[...] = is_place.astype(f32).astype(bf16)
    pick_shift = (sub16 == 2 * request).astype(f32)
    pick_scale = (sub16 == 2 * request + 1).astype(f32)

    def second_hop(t):
        arrived(relay.at[t, 0:ROLES, 1:SLOTS_PER_STEP], S_HOP + t)
        for d in (1, 3, 2, 0):

            @pl.when(role_at(x, y + d) < ROLES)
            def _(d=d):
                own_hop(t, d).wait()
                if d > 0:
                    send(relay.at[t, d], final.at[t, d], S_LAST + NY * t + d, y_peer(d))

    arrived(md.at[1:NY], S_MOD)
    arrived(stats.at[1:PLANE], S_STAT)
    summed = stats[0]
    for i in range(1, PLANE):
        summed = summed + stats[i]
    mean = summed[0:1] / D
    power = summed[1:2] / D
    scaled = lax.rsqrt(power - mean * mean + 1e-06)
    over_rows = (((0,), (0,)), ((), ()))
    arrived(tx.at[1:NY], S_TEXT)
    for d in range(NY):
        shift = lax.dot_general(
            md[d], pick_shift, over_rows, precision=lax.Precision.HIGHEST, preferred_element_type=f32
        )
        scale = lax.dot_general(
            md[d], pick_scale, over_rows, precision=lax.Precision.HIGHEST, preferred_element_type=f32
        )
        shaped = (tx[d].astype(f32) - mean) * scaled * (1.0 + scale) + shift
        xs[d] = shaped.astype(bf16)

    second_hop(0)
    second_hop(1)
    for part in range(2):
        arrived(w.at[part, 1:NY, half], S_W + part)
        send(w.at[part, 1:NY, half], w.at[part, 1:NY, half], S_WC + part, sibling)

    second_hop(2)
    for part, copy in ((0, own_wk), (1, own_wv)):
        copy.wait()
        arrived(w.at[part, 1:NY, half], S_WC + part)
        acc[part] = lax.dot_general(
            xs[...].reshape(D // NX, ROWS), w[part].reshape(D // NX, WIDE), over_rows,
            preferred_element_type=f32,
        )
        sum_s[part] = acc[part].astype(bf16)
        for d in range(1, NX):
            its_role = lax.rem(x + d + y, NX)

            @pl.when(its_role < ROLES)
            def _(part=part, d=d, its_role=its_role):
                src = sum_s.at[part, :, head_columns(its_role)]
                send(src, sum_r.at[part, d], S_SUM + part, x_peer(d))

    @pl.when(active)
    def _():
        over_columns = (((1,), (1,)), ((), ()))

        def flatten(block):
            return block.astype(f32).reshape(STEP, HEAD_DIM).astype(bf16)

        def update(lanes, s, values, first):
            newest = jnp.max(s, axis=0, keepdims=True)
            if not first:
                newest = jnp.maximum(m[:, lanes], newest)
            weights = jnp.exp2((s - newest) * FACTOR)
            total = jnp.sum(weights, axis=0, keepdims=True)
            mixed = lax.dot_general(values, weights.astype(bf16), over_rows, preferred_element_type=f32)
            if not first:
                fade = jnp.exp2((m[:, lanes] - newest) * FACTOR)
                total = l[:, lanes] * fade + total
                mixed = o[:, lanes] * fade + mixed
            m[:, lanes] = newest
            l[:, lanes] = total
            o[:, lanes] = mixed

        def image_chunk(c):
            for t, dst in ((1, kh), (2, vh)):
                if c > 0:
                    arrived(final.at[t, c], S_LAST + NY * t + c)
                dst[...] = flatten((final if c > 0 else relay)[t, c])

            def image_step(b, carry):
                lanes = pl.ds(pl.multiple_of(b * LANES, LANES), LANES)
                s = lax.dot_general(kh[...], qh[lanes, :], over_columns, preferred_element_type=f32)
                update(lanes, s, vh[...], c == 0)
                return carry

            lax.fori_loop(0, IMG // LANES, image_step, 0)

        for d in (0, 1, 3, 2):
            if d > 0:
                arrived(final.at[0, d], S_LAST + d)
            qh[pl.ds(d * STEP, STEP), :] = flatten((final if d > 0 else relay)[0, d])
        image_chunk(0)

        for part in range(2):
            arrived(sum_r.at[part, 1:NX], S_SUM + part)
            rows = acc[part, :, head_columns(role)]
            for d in range(1, NX):
                rows = rows + sum_r[part, d].astype(f32)
            moved = jnp.dot(place_t[...], rows.astype(bf16), preferred_element_type=f32)
            rep_s[part] = moved.astype(bf16).reshape(REPS, SLOTS, HEAD_DIM)
            for d in range(1, REPS):
                src = rep_s.at[part, lax.rem(rep + d, REPS)]
                send(src, landed.at[part, d], S_REP + part, rep_peer(d))
            landed[part, 0] = rep_s[part, rep]

        image_chunk(1)
        image_chunk(3)
        image_chunk(2)


        arrived(rq.at[1:REPS], S_REQ)
        named = jnp.concatenate([rq[d] for d in range(REPS)], axis=0) == rep
        counted = jnp.sum(jnp.where(named, 1.0, 0.0), axis=1, keepdims=True)
        slot_number = lax.broadcasted_iota(jnp.int32, (SLOTS, HEAD_DIM), 0).astype(f32)
        live = jnp.concatenate([slot_number < counted[d : d + 1] for d in range(REPS)], axis=0)

        for part in range(2):
            arrived(landed.at[part, 1:REPS], S_REP + part)

        def text_step(b, carry):
            lanes = pl.ds(pl.multiple_of(b * LANES, LANES), LANES)
            keys = landed[0].reshape(TEXT, HEAD_DIM)
            values = landed[1].reshape(TEXT, HEAD_DIM)
            s = lax.dot_general(keys, qh[lanes, :], over_columns, preferred_element_type=f32)
            update(lanes, jnp.where(live[:, 0:1], s, LOWEST), values, False)
            result = (o[:, lanes] / l[:, lanes]).T.reshape(SLOTS_A_STEP, IMG_DEV, HEAD_DIM)
            o_s[pl.ds(b * SLOTS_A_STEP, SLOTS_A_STEP)] = result.astype(bf16)

            def send_result(k, inner):
                i = b * SLOTS_A_STEP + k

                @pl.when(i > 0)
                def _():
                    send(o_s.at[i], out.at[0, :, own_head], S_OUT, group_at(*behind(i)))

                return inner

            lax.fori_loop(0, SLOTS_A_STEP, send_result, 0)
            return carry

        lax.fori_loop(0, IMG // LANES, text_step, 0)
        last = pltpu.make_async_copy(o_s.at[0], out.at[0, :, own_head], lsem.at[17])
        last.start()
        arrived(out.at[0, :, 0 : (NY * NZ * ROLES - 1) * HEAD_DIM], S_OUT)
        last.wait()
        left(o_s.at[1:GROUP], S_OUT)
        for part in range(2):
            left(sum_r.at[part, 1 : NX - 1], S_SUM + part)
            left(landed.at[part, 1:REPS], S_REP + part)

    @pl.when(idle)
    def _():
        arrived(rq.at[1:REPS], S_REQ)
        arrived(out.at[0], S_OUT)
        for part in range(2):
            left(sum_r.at[part, 1:NX], S_SUM + part)

    for t in range(3):
        left(relay.at[t, 0:ROLES, 1:SLOTS_PER_STEP], S_HOP + t)
        for d in range(1, NY):

            @pl.when(role_at(x, y + d) < ROLES)
            def _(t=t, d=d):
                left(relay.at[t, d], S_LAST + NY * t + d)

    left(tx.at[1:NY], S_TEXT)
    left(md.at[1:NY], S_MOD)
    left(stats.at[1:PLANE], S_STAT)
    left(rq.at[1:REPS], S_REQ)
    for part in range(2):
        left(w.at[part, 1:NY, half], S_W + part)
        left(w.at[part, 1:NY, half], S_WC + part)


def local(text_rows, modulation, timestep, row_request, w_key, w_value, q_image, k_image, v_image):
    f32, bf16 = jnp.float32, jnp.bfloat16
    smem = pl.BlockSpec(memory_space=pltpu.SMEM)
    hbm = pl.BlockSpec(memory_space=pl.ANY)
    features = text_rows.shape[1]
    blocks = pltpu.VMEM((GROUP, IMG_DEV, HEAD_DIM), bf16)
    hops = pltpu.VMEM((3, NY, SLOTS_PER_STEP, IMG_DEV, HEAD_DIM), bf16)
    return pl.pallas_call(
        kernel,
        out_shape=jax.ShapeDtypeStruct(q_image.shape, bf16),
        in_specs=[hbm, hbm, smem, hbm, hbm, hbm, hbm, hbm, hbm],
        out_specs=hbm,
        scratch_shapes=[
            pltpu.VMEM((NY, features, ROWS), bf16),
            pltpu.VMEM(modulation.shape, f32),
            pltpu.VMEM((NY, 2 * REPS, features), f32),
            pltpu.VMEM((REPS, 1, ROWS), jnp.int32),
            pltpu.VMEM((2, NY, features, WIDE), bf16),
            hops,
            hops,
            pltpu.VMEM((PLANE, 8, ROWS), f32),
            pltpu.VMEM((NY, features, ROWS), bf16),
            pltpu.VMEM((2, ROWS, WIDE), f32),
            pltpu.VMEM((2, ROWS, WIDE), bf16),
            pltpu.VMEM((2, NX, ROWS, HEAD_DIM), bf16),
            pltpu.VMEM((TEXT, ROWS), bf16),
            pltpu.VMEM((2, REPS, SLOTS, HEAD_DIM), bf16),
            pltpu.VMEM((2, REPS, SLOTS, HEAD_DIM), bf16),
            pltpu.VMEM((IMG, HEAD_DIM), bf16),
            pltpu.VMEM((STEP, HEAD_DIM), bf16),
            pltpu.VMEM((STEP, HEAD_DIM), bf16),
            pltpu.VMEM((1, IMG), f32),
            pltpu.VMEM((1, IMG), f32),
            pltpu.VMEM((HEAD_DIM, IMG), f32),
            blocks,
            pltpu.SemaphoreType.DMA((S_ALL,)),
            pltpu.SemaphoreType.DMA((S_ALL,)),
            pltpu.SemaphoreType.DMA((18,)),
        ],
        compiler_params=pltpu.CompilerParams(
            collective_id=0, has_side_effects=True, vmem_limit_bytes=VMEM_LIMIT
        ),
    )(
        text_rows.T, modulation, timestep, row_request.reshape(1, -1),
        w_key, w_value, q_image, k_image, v_image,
    )


def solution(mesh):
    image = P("rep", ("seq", "chip"), None)
    return jax.shard_map(
        local,
        mesh=mesh,
        in_specs=(
            P("rep", "seq"),
            P(None, None, "seq"),
            P(),
            P("rep", None),
            P("seq", "chip"),
            P("seq", "chip"),
            image,
            image,
            image,
        ),
        out_specs=image,
        check_vma=False,
    )
```

```python
import math

import jax
import jax.numpy as jnp
from jax import lax
from jax.experimental import pallas as pl
from jax.experimental.pallas import tpu as pltpu
from jax.sharding import PartitionSpec as P

D = 3072
HEAD_DIM = 128
CAP = 4
BLOCK = 16
NX = 4
NY = 4
NZ = 2
REPS = 8
PLANE = NX * NY
GROUP = PLANE * NZ
ROLES = 3
WIDE = ROLES * HEAD_DIM
IMG_DEV = 56
IMG = GROUP * IMG_DEV
SLOTS_PER_STEP = 8
STEP = SLOTS_PER_STEP * IMG_DEV
LANES = 896
SLOTS_A_STEP = LANES // IMG_DEV
ROWS = 256
SLOTS = ROWS // BLOCK * CAP
TEXT = REPS * SLOTS
HALF = 96
FACTOR = math.log2(math.e) / math.sqrt(HEAD_DIM)
LOWEST = -1e30
VMEM_LIMIT = 60 * 1024 * 1024
MESH = pl.DeviceIdType.MESH

S_TEXT, S_MOD, S_STAT, S_REQ = 0, 1, 2, 3
S_W, S_WC, S_SUM, S_REP = 4, 6, 8, 10
S_OUT, S_HOP, S_LAST = 12, 13, 16
S_ALL = 28


def kernel(
    text, mod, step, req, w_key, w_value, q_in, k_in, v_in, out,
    tx, mod_v, md, rq, w, relay, final, stats, xs, acc, sum_s, sum_r,
    place_t, rep_s, landed, qh, kh, vh, m, l, o, o_s,
    ssem, rsem, lsem,
):
    f32, bf16 = jnp.float32, jnp.bfloat16
    rep, seq, z = lax.axis_index("rep"), lax.axis_index("seq"), lax.axis_index("chip")
    y, x = lax.div(seq, NX), lax.rem(seq, NX)
    role = lax.rem(x + y, NX)
    active = role < ROLES
    idle = role >= ROLES

    def group_at(px, py, pz):
        return (rep, py * NX + px, pz)

    def offsets(i):
        return lax.rem(i, NX), lax.div(i, SLOTS_PER_STEP), lax.rem(lax.div(i, NX), NZ)

    def ahead(i):
        dx, dy, dz = offsets(i)
        return lax.rem(x + dx, NX), lax.rem(y + dy, NY), lax.rem(z + dz, NZ)

    def behind(i):
        dx, dy, dz = offsets(i)
        return lax.rem(x + NX - dx, NX), lax.rem(y + NY - dy, NY), lax.rem(z + NZ - dz, NZ)

    def x_peer(d):
        return (rep, y * NX + lax.rem(x + d, NX), z)

    def y_peer(d):
        return (rep, lax.rem(y + d, NY) * NX + x, z)

    def rep_peer(d):
        return (lax.rem(rep + d, REPS), seq, z)

    def head_columns(head):
        return pl.ds(pl.multiple_of(head * HEAD_DIM, HEAD_DIM), HEAD_DIM)

    def columns(index):
        return pl.ds(pl.multiple_of(index * WIDE, WIDE), WIDE)

    own_head = head_columns((z * NY + y) * ROLES + role)

    def remote(src, dst, index, peer):
        return pltpu.make_async_remote_copy(
            src_ref=src, dst_ref=dst, send_sem=ssem.at[index], recv_sem=rsem.at[index],
            device_id=peer, device_id_type=MESH,
        )

    def send(src, dst, index, peer):
        remote(src, dst, index, peer).start()

    def arrived(ref, index):
        remote(ref, ref, index, x_peer(1)).wait_recv()

    def left(ref, index):
        remote(ref, ref, index, x_peer(1)).wait_send()

    barrier = pltpu.get_barrier_semaphore()

    def greet(i, carry):
        pl.semaphore_signal(barrier, inc=1, device_id=group_at(*ahead(i)), device_id_type=MESH)
        return carry

    lax.fori_loop(1, GROUP, greet, 0)
    for d in range(1, REPS):
        pl.semaphore_signal(barrier, inc=1, device_id=rep_peer(d), device_id_type=MESH)

    own = [
        pltpu.make_async_copy(text, tx.at[0], lsem.at[0]),
        pltpu.make_async_copy(mod, mod_v, lsem.at[1]),
        pltpu.make_async_copy(req, rq.at[0], lsem.at[2]),
        pltpu.make_async_copy(w_key.at[:, columns(y)], w.at[0, 0], lsem.at[3]),
        pltpu.make_async_copy(w_value.at[:, columns(y)], w.at[1, 0], lsem.at[4]),
    ]
    own_text, own_mod, own_req, own_wk, own_wv = own
    for copy in own:
        copy.start()
    def role_at(px, py):
        return lax.rem(px + py, NX)

    def head_at(px, py, pz):
        return head_columns((pz * NY + py) * ROLES + role_at(px, py))

    image = (q_in, k_in, v_in)

    def own_hop(t, d):
        py = lax.rem(y + d, NY)
        return pltpu.make_async_copy(
            image[t].at[0, :, head_at(x, py, z)], relay.at[t, d, 0], lsem.at[5 + NY * t + d]
        )

    for d in range(NY):

        @pl.when(role_at(x, y + d) < ROLES)
        def _(d=d):
            for t in range(3):
                own_hop(t, d).start()

    pl.semaphore_wait(barrier, GROUP - 1 + REPS - 1)

    for d in range(1, NY):
        send(text, tx.at[d], S_TEXT, y_peer(d))

    own_mod.wait()
    for g in range(REPS):
        md[0, 2 * g : 2 * g + 2, :] = mod_v[step[g]]
    for d in range(1, NY):
        send(md.at[0], md.at[d], S_MOD, y_peer(d))

    own_text.wait()
    part = tx[0].astype(f32)
    stats[0] = jnp.concatenate(
        [
            jnp.sum(part, axis=0, keepdims=True),
            jnp.sum(part * part, axis=0, keepdims=True),
            jnp.zeros((6, ROWS), f32),
        ],
        axis=0,
    )

    def send_stats(i, carry):
        px, py = lax.rem(x + lax.rem(i, NX), NX), lax.rem(y + lax.div(i, NX), NY)
        send(stats.at[0], stats.at[i], S_STAT, group_at(px, py, z))
        return carry

    lax.fori_loop(1, PLANE, send_stats, 0)

    core = lax.rem(rep, 2)
    sibling = (rep + 1 - 2 * core, seq, z)
    half = pl.ds(pl.multiple_of(core * HALF, HALF), HALF)
    for part, src in ((0, w_key), (1, w_value)):
        for d in range(1, NY):
            there = columns(lax.rem(y + d, NY))
            send(src.at[half, there], w.at[part, d, half], S_W + part, y_peer(d))

    for t in range(3):

        def first_hop(n, carry, t=t):
            i = lax.rem(n, SLOTS_PER_STEP - 1) + 1
            d = lax.div(n, SLOTS_PER_STEP - 1)
            px, _, pz = ahead(i)
            py = lax.rem(y + d, NY)

            @pl.when(role_at(px, py) < ROLES)
            def _():
                send(image[t].at[0, :, head_at(px, py, pz)], relay.at[t, d, i], S_HOP + t, group_at(px, y, pz))

            return carry

        lax.fori_loop(0, NY * (SLOTS_PER_STEP - 1), first_hop, 0)
    for d in range(1, REPS):
        send(req, rq.at[d], S_REQ, rep_peer(d))

    own_req.wait()
    request = rq[0]
    sub16 = lax.broadcasted_iota(jnp.int32, (16, ROWS), 0)
    is_target = sub16 == request
    first_row = lax.broadcasted_iota(jnp.int32, (ROWS, ROWS), 0)
    second_row = lax.broadcasted_iota(jnp.int32, (ROWS, ROWS), 1)
    earlier = (first_row < second_row).astype(f32).astype(bf16)
    count = jnp.dot(is_target.astype(f32).astype(bf16), earlier, preferred_element_type=f32)
    slot = jnp.sum(jnp.where(is_target, count, 0.0), axis=0, keepdims=True).astype(jnp.int32)
    is_place = lax.broadcasted_iota(jnp.int32, (TEXT, ROWS), 0) == request * SLOTS + slot
    place_t[...] = is_place.astype(f32).astype(bf16)
    pick_shift = (sub16 == 2 * request).astype(f32)
    pick_scale = (sub16 == 2 * request + 1).astype(f32)

    def second_hop(t):
        arrived(relay.at[t, 0:ROLES, 1:SLOTS_PER_STEP], S_HOP + t)
        for d in (1, 3, 2, 0):

            @pl.when(role_at(x, y + d) < ROLES)
            def _(d=d):
                own_hop(t, d).wait()
                if d > 0:
                    send(relay.at[t, d], final.at[t, d], S_LAST + NY * t + d, y_peer(d))

    arrived(md.at[1:NY], S_MOD)
    arrived(stats.at[1:PLANE], S_STAT)
    summed = stats[0]
    for i in range(1, PLANE):
        summed = summed + stats[i]
    mean = summed[0:1] / D
    power = summed[1:2] / D
    scaled = lax.rsqrt(power - mean * mean + 1e-06)
    over_rows = (((0,), (0,)), ((), ()))
    arrived(tx.at[1:NY], S_TEXT)
    for d in range(NY):
        shift = lax.dot_general(
            md[d], pick_shift, over_rows, precision=lax.Precision.HIGHEST, preferred_element_type=f32
        )
        scale = lax.dot_general(
            md[d], pick_scale, over_rows, precision=lax.Precision.HIGHEST, preferred_element_type=f32
        )
        shaped = (tx[d].astype(f32) - mean) * scaled * (1.0 + scale) + shift
        xs[d] = shaped.astype(bf16)

    second_hop(0)
    for part in range(2):
        arrived(w.at[part, 1:NY, half], S_W + part)
        send(w.at[part, 1:NY, half], w.at[part, 1:NY, half], S_WC + part, sibling)

    for part, copy in ((0, own_wk), (1, own_wv)):
        copy.wait()
        arrived(w.at[part, 1:NY, half], S_WC + part)
        acc[part] = lax.dot_general(
            xs[...].reshape(D // NX, ROWS), w[part].reshape(D // NX, WIDE), over_rows,
            preferred_element_type=f32,
        )
        sum_s[part] = acc[part].astype(bf16)
        for d in range(1, NX):
            its_role = lax.rem(x + d + y, NX)

            @pl.when(its_role < ROLES)
            def _(part=part, d=d, its_role=its_role):
                src = sum_s.at[part, :, head_columns(its_role)]
                send(src, sum_r.at[part, d], S_SUM + part, x_peer(d))

    second_hop(1)
    second_hop(2)

    @pl.when(active)
    def _():
        over_columns = (((1,), (1,)), ((), ()))

        def flatten(block):
            return block.astype(f32).reshape(STEP, HEAD_DIM).astype(bf16)

        def update(lanes, s, values, first):
            newest = jnp.max(s, axis=0, keepdims=True)
            if not first:
                newest = jnp.maximum(m[:, lanes], newest)
            weights = jnp.exp2((s - newest) * FACTOR)
            total = jnp.sum(weights, axis=0, keepdims=True)
            mixed = lax.dot_general(values, weights.astype(bf16), over_rows, preferred_element_type=f32)
            if not first:
                fade = jnp.exp2((m[:, lanes] - newest) * FACTOR)
                total = l[:, lanes] * fade + total
                mixed = o[:, lanes] * fade + mixed
            m[:, lanes] = newest
            l[:, lanes] = total
            o[:, lanes] = mixed

        def image_chunk(c):
            for t, dst in ((1, kh), (2, vh)):
                if c > 0:
                    arrived(final.at[t, c], S_LAST + NY * t + c)
                dst[...] = flatten((final if c > 0 else relay)[t, c])

            def image_step(b, carry):
                lanes = pl.ds(pl.multiple_of(b * LANES, LANES), LANES)
                s = lax.dot_general(kh[...], qh[lanes, :], over_columns, preferred_element_type=f32)
                update(lanes, s, vh[...], c == 0)
                return carry

            lax.fori_loop(0, IMG // LANES, image_step, 0)

        for d in (0, 1, 3, 2):
            if d > 0:
                arrived(final.at[0, d], S_LAST + d)
            qh[pl.ds(d * STEP, STEP), :] = flatten((final if d > 0 else relay)[0, d])
        image_chunk(0)

        for part in range(2):
            arrived(sum_r.at[part, 1:NX], S_SUM + part)
            rows = acc[part, :, head_columns(role)]
            for d in range(1, NX):
                rows = rows + sum_r[part, d].astype(f32)
            moved = jnp.dot(place_t[...], rows.astype(bf16), preferred_element_type=f32)
            rep_s[part] = moved.astype(bf16).reshape(REPS, SLOTS, HEAD_DIM)
            for d in range(1, REPS):
                src = rep_s.at[part, lax.rem(rep + d, REPS)]
                send(src, landed.at[part, d], S_REP + part, rep_peer(d))
            landed[part, 0] = rep_s[part, rep]

        image_chunk(1)
        image_chunk(3)
        image_chunk(2)


        arrived(rq.at[1:REPS], S_REQ)
        named = jnp.concatenate([rq[d] for d in range(REPS)], axis=0) == rep
        counted = jnp.sum(jnp.where(named, 1.0, 0.0), axis=1, keepdims=True)
        slot_number = lax.broadcasted_iota(jnp.int32, (SLOTS, HEAD_DIM), 0).astype(f32)
        live = jnp.concatenate([slot_number < counted[d : d + 1] for d in range(REPS)], axis=0)

        for part in range(2):
            arrived(landed.at[part, 1:REPS], S_REP + part)

        def text_step(n, carry):
            b = IMG // LANES - 1 - n
            lanes = pl.ds(pl.multiple_of(b * LANES, LANES), LANES)
            keys = landed[0].reshape(TEXT, HEAD_DIM)
            values = landed[1].reshape(TEXT, HEAD_DIM)
            s = lax.dot_general(keys, qh[lanes, :], over_columns, preferred_element_type=f32)
            update(lanes, jnp.where(live[:, 0:1], s, LOWEST), values, False)
            result = (o[:, lanes] / l[:, lanes]).T.reshape(SLOTS_A_STEP, IMG_DEV, HEAD_DIM)
            o_s[pl.ds(b * SLOTS_A_STEP, SLOTS_A_STEP)] = result.astype(bf16)

            def send_result(k, inner):
                i = b * SLOTS_A_STEP + SLOTS_A_STEP - 1 - k

                @pl.when(i > 0)
                def _():
                    send(o_s.at[i], out.at[0, :, own_head], S_OUT, group_at(*behind(i)))

                return inner

            lax.fori_loop(0, SLOTS_A_STEP, send_result, 0)
            return carry

        lax.fori_loop(0, IMG // LANES, text_step, 0)
        last = pltpu.make_async_copy(o_s.at[0], out.at[0, :, own_head], lsem.at[17])
        last.start()
        arrived(out.at[0, :, 0 : (NY * NZ * ROLES - 1) * HEAD_DIM], S_OUT)
        last.wait()
        left(o_s.at[1:GROUP], S_OUT)
        for part in range(2):
            left(sum_r.at[part, 1 : NX - 1], S_SUM + part)
            left(landed.at[part, 1:REPS], S_REP + part)

    @pl.when(idle)
    def _():
        arrived(rq.at[1:REPS], S_REQ)
        arrived(out.at[0], S_OUT)
        for part in range(2):
            left(sum_r.at[part, 1:NX], S_SUM + part)

    for t in range(3):
        left(relay.at[t, 0:ROLES, 1:SLOTS_PER_STEP], S_HOP + t)
        for d in range(1, NY):

            @pl.when(role_at(x, y + d) < ROLES)
            def _(t=t, d=d):
                left(relay.at[t, d], S_LAST + NY * t + d)

    left(tx.at[1:NY], S_TEXT)
    left(md.at[1:NY], S_MOD)
    left(stats.at[1:PLANE], S_STAT)
    left(rq.at[1:REPS], S_REQ)
    for part in range(2):
        left(w.at[part, 1:NY, half], S_W + part)
        left(w.at[part, 1:NY, half], S_WC + part)


def local(text_rows, modulation, timestep, row_request, w_key, w_value, q_image, k_image, v_image):
    f32, bf16 = jnp.float32, jnp.bfloat16
    smem = pl.BlockSpec(memory_space=pltpu.SMEM)
    hbm = pl.BlockSpec(memory_space=pl.ANY)
    features = text_rows.shape[1]
    blocks = pltpu.VMEM((GROUP, IMG_DEV, HEAD_DIM), bf16)
    hops = pltpu.VMEM((3, NY, SLOTS_PER_STEP, IMG_DEV, HEAD_DIM), bf16)
    return pl.pallas_call(
        kernel,
        out_shape=jax.ShapeDtypeStruct(q_image.shape, bf16),
        in_specs=[hbm, hbm, smem, hbm, hbm, hbm, hbm, hbm, hbm],
        out_specs=hbm,
        scratch_shapes=[
            pltpu.VMEM((NY, features, ROWS), bf16),
            pltpu.VMEM(modulation.shape, f32),
            pltpu.VMEM((NY, 2 * REPS, features), f32),
            pltpu.VMEM((REPS, 1, ROWS), jnp.int32),
            pltpu.VMEM((2, NY, features, WIDE), bf16),
            hops,
            hops,
            pltpu.VMEM((PLANE, 8, ROWS), f32),
            pltpu.VMEM((NY, features, ROWS), bf16),
            pltpu.VMEM((2, ROWS, WIDE), f32),
            pltpu.VMEM((2, ROWS, WIDE), bf16),
            pltpu.VMEM((2, NX, ROWS, HEAD_DIM), bf16),
            pltpu.VMEM((TEXT, ROWS), bf16),
            pltpu.VMEM((2, REPS, SLOTS, HEAD_DIM), bf16),
            pltpu.VMEM((2, REPS, SLOTS, HEAD_DIM), bf16),
            pltpu.VMEM((IMG, HEAD_DIM), bf16),
            pltpu.VMEM((STEP, HEAD_DIM), bf16),
            pltpu.VMEM((STEP, HEAD_DIM), bf16),
            pltpu.VMEM((1, IMG), f32),
            pltpu.VMEM((1, IMG), f32),
            pltpu.VMEM((HEAD_DIM, IMG), f32),
            blocks,
            pltpu.SemaphoreType.DMA((S_ALL,)),
            pltpu.SemaphoreType.DMA((S_ALL,)),
            pltpu.SemaphoreType.DMA((18,)),
        ],
        compiler_params=pltpu.CompilerParams(
            collective_id=0, has_side_effects=True, vmem_limit_bytes=VMEM_LIMIT
        ),
    )(
        text_rows.T, modulation, timestep, row_request.reshape(1, -1),
        w_key, w_value, q_image, k_image, v_image,
    )


def solution(mesh):
    image = P("rep", ("seq", "chip"), None)
    return jax.shard_map(
        local,
        mesh=mesh,
        in_specs=(
            P("rep", "seq"),
            P(None, None, "seq"),
            P(),
            P("rep", None),
            P("seq", "chip"),
            P("seq", "chip"),
            image,
            image,
            image,
        ),
        out_specs=image,
        check_vma=False,
    )
```

```python
import math

import jax
import jax.numpy as jnp
from jax import lax
from jax.experimental import pallas as pl
from jax.experimental.pallas import tpu as pltpu
from jax.sharding import PartitionSpec as P

D = 3072
HEAD_DIM = 128
CAP = 4
BLOCK = 16
NX = 4
NY = 4
NZ = 2
REPS = 8
PLANE = NX * NY
GROUP = PLANE * NZ
ROLES = 3
WIDE = ROLES * HEAD_DIM
IMG_DEV = 56
IMG = GROUP * IMG_DEV
SLOTS_PER_STEP = 8
STEP = SLOTS_PER_STEP * IMG_DEV
LANES = 896
SLOTS_A_STEP = LANES // IMG_DEV
ROWS = 256
SLOTS = ROWS // BLOCK * CAP
TEXT = REPS * SLOTS
FACTOR = math.log2(math.e) / math.sqrt(HEAD_DIM)
LOWEST = -1e30
VMEM_LIMIT = 60 * 1024 * 1024
MESH = pl.DeviceIdType.MESH

S_TEXT, S_MOD, S_STAT, S_REQ = 0, 1, 2, 3
S_W, S_WC, S_SUM, S_REP = 4, 6, 8, 10
S_OUT, S_HOP, S_LAST = 12, 13, 16
S_ALL = 28


def kernel(
    text, mod, step, req, w_key, w_value, q_in, k_in, v_in, out,
    tx, mod_v, md, rq, w, relay, final, stats, xs, acc, sum_s, sum_r,
    place_t, rep_s, landed, qh, kh, vh, m, l, o, o_s,
    ssem, rsem, lsem,
):
    f32, bf16 = jnp.float32, jnp.bfloat16
    rep, seq, z = lax.axis_index("rep"), lax.axis_index("seq"), lax.axis_index("chip")
    y, x = lax.div(seq, NX), lax.rem(seq, NX)
    role = lax.rem(x + y, NX)
    active = role < ROLES
    idle = role >= ROLES

    def group_at(px, py, pz):
        return (rep, py * NX + px, pz)

    def offsets(i):
        return lax.rem(i, NX), lax.div(i, SLOTS_PER_STEP), lax.rem(lax.div(i, NX), NZ)

    def ahead(i):
        dx, dy, dz = offsets(i)
        return lax.rem(x + dx, NX), lax.rem(y + dy, NY), lax.rem(z + dz, NZ)

    def behind(i):
        dx, dy, dz = offsets(i)
        return lax.rem(x + NX - dx, NX), lax.rem(y + NY - dy, NY), lax.rem(z + NZ - dz, NZ)

    def x_peer(d):
        return (rep, y * NX + lax.rem(x + d, NX), z)

    def y_peer(d):
        return (rep, lax.rem(y + d, NY) * NX + x, z)

    def rep_peer(d):
        return (lax.rem(rep + d, REPS), seq, z)

    def head_columns(head):
        return pl.ds(pl.multiple_of(head * HEAD_DIM, HEAD_DIM), HEAD_DIM)

    def columns(index):
        return pl.ds(pl.multiple_of(index * WIDE, WIDE), WIDE)

    own_head = head_columns((z * NY + y) * ROLES + role)

    def remote(src, dst, index, peer):
        return pltpu.make_async_remote_copy(
            src_ref=src, dst_ref=dst, send_sem=ssem.at[index], recv_sem=rsem.at[index],
            device_id=peer, device_id_type=MESH,
        )

    def send(src, dst, index, peer):
        remote(src, dst, index, peer).start()

    def arrived(ref, index):
        remote(ref, ref, index, x_peer(1)).wait_recv()

    def left(ref, index):
        remote(ref, ref, index, x_peer(1)).wait_send()

    barrier = pltpu.get_barrier_semaphore()

    def greet(i, carry):
        pl.semaphore_signal(barrier, inc=1, device_id=group_at(*ahead(i)), device_id_type=MESH)
        return carry

    lax.fori_loop(1, GROUP, greet, 0)
    for d in range(1, REPS):
        pl.semaphore_signal(barrier, inc=1, device_id=rep_peer(d), device_id_type=MESH)

    own = [
        pltpu.make_async_copy(text, tx.at[0], lsem.at[0]),
        pltpu.make_async_copy(mod, mod_v, lsem.at[1]),
        pltpu.make_async_copy(req, rq.at[rep], lsem.at[2]),
    ]
    own_text, own_mod, own_req = own
    for copy in own:
        copy.start()

    core = lax.rem(rep, 2)
    sibling = (rep + 1 - 2 * core, seq, z)
    both = rep - core

    def on_core(number, src, what):
        @pl.when(core == number)
        def _():
            what(src)

    def own_weights(src):
        return pltpu.make_async_copy(src.at[:, columns(y)], w.at[0], lsem.at[3])

    on_core(0, w_key, lambda src: own_weights(src).start())
    on_core(1, w_value, lambda src: own_weights(src).start())

    def role_at(px, py):
        return lax.rem(px + py, NX)

    def head_at(px, py, pz):
        return head_columns((pz * NY + py) * ROLES + role_at(px, py))

    image = (q_in, k_in, v_in)

    def own_hop(t, d):
        py = lax.rem(y + d, NY)
        return pltpu.make_async_copy(
            image[t].at[0, :, head_at(x, py, z)], relay.at[t, d, 0], lsem.at[5 + NY * t + d]
        )

    for d in range(NY):

        @pl.when(role_at(x, y + d) < ROLES)
        def _(d=d):
            for t in range(3):
                own_hop(t, d).start()

    pl.semaphore_wait(barrier, GROUP - 1 + REPS - 1)

    for d in range(1, NY):
        send(text, tx.at[d], S_TEXT, y_peer(d))

    own_mod.wait()
    for g in range(REPS):
        md[0, 2 * g : 2 * g + 2, :] = mod_v[step[g]]
    for d in range(1, NY):
        send(md.at[0], md.at[d], S_MOD, y_peer(d))

    own_text.wait()
    part = tx[0].astype(f32)
    stats[0] = jnp.concatenate(
        [
            jnp.sum(part, axis=0, keepdims=True),
            jnp.sum(part * part, axis=0, keepdims=True),
            jnp.zeros((6, ROWS), f32),
        ],
        axis=0,
    )

    def send_stats(i, carry):
        px, py = lax.rem(x + lax.rem(i, NX), NX), lax.rem(y + lax.div(i, NX), NY)
        send(stats.at[0], stats.at[i], S_STAT, group_at(px, py, z))
        return carry

    lax.fori_loop(1, PLANE, send_stats, 0)

    def send_weights(src):
        for d in range(1, NY):
            send(src.at[:, columns(lax.rem(y + d, NY))], w.at[d], S_W, y_peer(d))

    on_core(0, w_key, send_weights)
    on_core(1, w_value, send_weights)

    for t in range(3):

        def first_hop(n, carry, t=t):
            i = lax.rem(n, SLOTS_PER_STEP - 1) + 1
            d = lax.div(n, SLOTS_PER_STEP - 1)
            px, _, pz = ahead(i)
            py = lax.rem(y + d, NY)

            @pl.when(role_at(px, py) < ROLES)
            def _():
                send(image[t].at[0, :, head_at(px, py, pz)], relay.at[t, d, i], S_HOP + t, group_at(px, y, pz))

            return carry

        lax.fori_loop(0, NY * (SLOTS_PER_STEP - 1), first_hop, 0)
    for d in range(1, REPS):
        send(req, rq.at[rep], S_REQ, rep_peer(d))

    own_req.wait()
    request = rq[rep]
    sub16 = lax.broadcasted_iota(jnp.int32, (16, ROWS), 0)
    pick_shift = (sub16 == 2 * request).astype(f32)
    pick_scale = (sub16 == 2 * request + 1).astype(f32)

    def second_hop(t):
        arrived(relay.at[t, 0:ROLES, 1:SLOTS_PER_STEP], S_HOP + t)
        for d in (1, 3, 2, 0):

            @pl.when(role_at(x, y + d) < ROLES)
            def _(d=d):
                own_hop(t, d).wait()
                if d > 0:
                    send(relay.at[t, d], final.at[t, d], S_LAST + NY * t + d, y_peer(d))

    arrived(md.at[1:NY], S_MOD)
    arrived(stats.at[1:PLANE], S_STAT)
    summed = stats[0]
    for i in range(1, PLANE):
        summed = summed + stats[i]
    mean = summed[0:1] / D
    power = summed[1:2] / D
    scaled = lax.rsqrt(power - mean * mean + 1e-06)
    over_rows = (((0,), (0,)), ((), ()))
    arrived(tx.at[1:NY], S_TEXT)
    for d in range(NY):
        shift = lax.dot_general(
            md[d], pick_shift, over_rows, precision=lax.Precision.HIGHEST, preferred_element_type=f32
        )
        scale = lax.dot_general(
            md[d], pick_scale, over_rows, precision=lax.Precision.HIGHEST, preferred_element_type=f32
        )
        shaped = (tx[d].astype(f32) - mean) * scaled * (1.0 + scale) + shift
        xs[core, d] = shaped.astype(bf16)
    send(xs.at[core], xs.at[core], S_WC, sibling)

    second_hop(0)
    arrived(w.at[1:NY], S_W)
    on_core(0, w_key, lambda src: own_weights(src).wait())
    on_core(1, w_value, lambda src: own_weights(src).wait())
    arrived(xs.at[0], S_WC)
    for part in range(2):
        acc[part] = lax.dot_general(
            xs[part].reshape(D // NX, ROWS), w[...].reshape(D // NX, WIDE), over_rows,
            preferred_element_type=f32,
        )
        sum_s[part] = acc[part].astype(bf16)
        for d in range(1, NX):
            its_role = lax.rem(x + d + y, NX)

            @pl.when(its_role < ROLES)
            def _(part=part, d=d, its_role=its_role):
                src = sum_s.at[part, :, head_columns(its_role)]
                send(src, sum_r.at[part, d], S_SUM + part, x_peer(d))

    second_hop(1)
    second_hop(2)

    arrived(rq.at[1:REPS], S_REQ)
    first_row = lax.broadcasted_iota(jnp.int32, (ROWS, ROWS), 0)
    second_row = lax.broadcasted_iota(jnp.int32, (ROWS, ROWS), 1)
    earlier = (first_row < second_row).astype(f32).astype(bf16)
    for part in range(2):
        request = rq[both + part]
        is_target = sub16 == request
        count = jnp.dot(is_target.astype(f32).astype(bf16), earlier, preferred_element_type=f32)
        slot = jnp.sum(jnp.where(is_target, count, 0.0), axis=0, keepdims=True).astype(jnp.int32)
        is_place = lax.broadcasted_iota(jnp.int32, (TEXT, ROWS), 0) == request * SLOTS + slot
        place_t[part] = is_place.astype(f32).astype(bf16)

    @pl.when(active)
    def _():
        over_columns = (((1,), (1,)), ((), ()))

        def flatten(block):
            return block.astype(f32).reshape(STEP, HEAD_DIM).astype(bf16)

        def update(lanes, s, values, first):
            newest = jnp.max(s, axis=0, keepdims=True)
            if not first:
                newest = jnp.maximum(m[:, lanes], newest)
            weights = jnp.exp2((s - newest) * FACTOR)
            total = jnp.sum(weights, axis=0, keepdims=True)
            mixed = lax.dot_general(values, weights.astype(bf16), over_rows, preferred_element_type=f32)
            if not first:
                fade = jnp.exp2((m[:, lanes] - newest) * FACTOR)
                total = l[:, lanes] * fade + total
                mixed = o[:, lanes] * fade + mixed
            m[:, lanes] = newest
            l[:, lanes] = total
            o[:, lanes] = mixed

        def image_chunk(c):
            for t, dst in ((1, kh), (2, vh)):
                if c > 0:
                    arrived(final.at[t, c], S_LAST + NY * t + c)
                dst[...] = flatten((final if c > 0 else relay)[t, c])

            def image_step(b, carry):
                lanes = pl.ds(pl.multiple_of(b * LANES, LANES), LANES)
                s = lax.dot_general(kh[...], qh[lanes, :], over_columns, preferred_element_type=f32)
                update(lanes, s, vh[...], c == 0)
                return carry

            lax.fori_loop(0, IMG // LANES, image_step, 0)

        for d in (0, 1, 3, 2):
            if d > 0:
                arrived(final.at[0, d], S_LAST + d)
            qh[pl.ds(d * STEP, STEP), :] = flatten((final if d > 0 else relay)[0, d])

        for part in range(2):
            arrived(sum_r.at[part, 1:NX], S_SUM + part)
            rows = acc[part, :, head_columns(role)]
            for d in range(1, NX):
                rows = rows + sum_r[part, d].astype(f32)
            moved = jnp.dot(place_t[part], rows.astype(bf16), preferred_element_type=f32)
            rep_s[part] = moved.astype(bf16).reshape(REPS, SLOTS, HEAD_DIM)
            for d in range(1, REPS):
                src = rep_s.at[part, lax.rem(rep + d, REPS)]
                send(src, landed.at[core, both + part], S_REP, rep_peer(d))
            landed[core, both + part] = rep_s[part, rep]

        image_chunk(0)
        image_chunk(3)
        image_chunk(1)
        image_chunk(2)


        named = jnp.concatenate([rq[d] for d in range(REPS)], axis=0) == rep
        counted = jnp.sum(jnp.where(named, 1.0, 0.0), axis=1, keepdims=True)
        slot_number = lax.broadcasted_iota(jnp.int32, (SLOTS, HEAD_DIM), 0).astype(f32)
        live = jnp.concatenate([slot_number < counted[d : d + 1] for d in range(REPS)], axis=0)

        arrived(landed.at[0:2, 1:REPS], S_REP)

        def text_step(n, carry):
            b = IMG // LANES - 1 - n
            lanes = pl.ds(pl.multiple_of(b * LANES, LANES), LANES)
            keys = landed[0].reshape(TEXT, HEAD_DIM)
            values = landed[1].reshape(TEXT, HEAD_DIM)
            s = lax.dot_general(keys, qh[lanes, :], over_columns, preferred_element_type=f32)
            update(lanes, jnp.where(live[:, 0:1], s, LOWEST), values, False)
            result = (o[:, lanes] / l[:, lanes]).T.reshape(SLOTS_A_STEP, IMG_DEV, HEAD_DIM)
            o_s[pl.ds(b * SLOTS_A_STEP, SLOTS_A_STEP)] = result.astype(bf16)

            def send_result(k, inner):
                i = b * SLOTS_A_STEP + SLOTS_A_STEP - 1 - k

                @pl.when(i > 0)
                def _():
                    send(o_s.at[i], out.at[0, :, own_head], S_OUT, group_at(*behind(i)))

                return inner

            lax.fori_loop(0, SLOTS_A_STEP, send_result, 0)
            return carry

        lax.fori_loop(0, IMG // LANES, text_step, 0)
        last = pltpu.make_async_copy(o_s.at[0], out.at[0, :, own_head], lsem.at[17])
        last.start()
        arrived(out.at[0, :, 0 : (NY * NZ * ROLES - 1) * HEAD_DIM], S_OUT)
        last.wait()
        left(o_s.at[1:GROUP], S_OUT)
        for part in range(2):
            left(sum_r.at[part, 1 : NX - 1], S_SUM + part)
        left(landed.at[0:2, 1:REPS], S_REP)

    @pl.when(idle)
    def _():
        arrived(out.at[0], S_OUT)
        for part in range(2):
            left(sum_r.at[part, 1:NX], S_SUM + part)

    for t in range(3):
        left(relay.at[t, 0:ROLES, 1:SLOTS_PER_STEP], S_HOP + t)
        for d in range(1, NY):

            @pl.when(role_at(x, y + d) < ROLES)
            def _(t=t, d=d):
                left(relay.at[t, d], S_LAST + NY * t + d)

    left(tx.at[1:NY], S_TEXT)
    left(md.at[1:NY], S_MOD)
    left(stats.at[1:PLANE], S_STAT)
    left(rq.at[1:REPS], S_REQ)
    left(w.at[1:NY], S_W)
    left(xs.at[0], S_WC)


def local(text_rows, modulation, timestep, row_request, w_key, w_value, q_image, k_image, v_image):
    f32, bf16 = jnp.float32, jnp.bfloat16
    smem = pl.BlockSpec(memory_space=pltpu.SMEM)
    hbm = pl.BlockSpec(memory_space=pl.ANY)
    features = text_rows.shape[1]
    blocks = pltpu.VMEM((GROUP, IMG_DEV, HEAD_DIM), bf16)
    hops = pltpu.VMEM((3, NY, SLOTS_PER_STEP, IMG_DEV, HEAD_DIM), bf16)
    return pl.pallas_call(
        kernel,
        out_shape=jax.ShapeDtypeStruct(q_image.shape, bf16),
        in_specs=[hbm, hbm, smem, hbm, hbm, hbm, hbm, hbm, hbm],
        out_specs=hbm,
        scratch_shapes=[
            pltpu.VMEM((NY, features, ROWS), bf16),
            pltpu.VMEM(modulation.shape, f32),
            pltpu.VMEM((NY, 2 * REPS, features), f32),
            pltpu.VMEM((REPS, 1, ROWS), jnp.int32),
            pltpu.VMEM((NY, features, WIDE), bf16),
            hops,
            hops,
            pltpu.VMEM((PLANE, 8, ROWS), f32),
            pltpu.VMEM((2, NY, features, ROWS), bf16),
            pltpu.VMEM((2, ROWS, WIDE), f32),
            pltpu.VMEM((2, ROWS, WIDE), bf16),
            pltpu.VMEM((2, NX, ROWS, HEAD_DIM), bf16),
            pltpu.VMEM((2, TEXT, ROWS), bf16),
            pltpu.VMEM((2, REPS, SLOTS, HEAD_DIM), bf16),
            pltpu.VMEM((2, REPS, SLOTS, HEAD_DIM), bf16),
            pltpu.VMEM((IMG, HEAD_DIM), bf16),
            pltpu.VMEM((STEP, HEAD_DIM), bf16),
            pltpu.VMEM((STEP, HEAD_DIM), bf16),
            pltpu.VMEM((1, IMG), f32),
            pltpu.VMEM((1, IMG), f32),
            pltpu.VMEM((HEAD_DIM, IMG), f32),
            blocks,
            pltpu.SemaphoreType.DMA((S_ALL,)),
            pltpu.SemaphoreType.DMA((S_ALL,)),
            pltpu.SemaphoreType.DMA((18,)),
        ],
        compiler_params=pltpu.CompilerParams(
            collective_id=0, has_side_effects=True, vmem_limit_bytes=VMEM_LIMIT
        ),
    )(
        text_rows.T, modulation, timestep, row_request.reshape(1, -1),
        w_key, w_value, q_image, k_image, v_image,
    )


def solution(mesh):
    image = P("rep", ("seq", "chip"), None)
    return jax.shard_map(
        local,
        mesh=mesh,
        in_specs=(
            P("rep", "seq"),
            P(None, None, "seq"),
            P(),
            P("rep", None),
            P("seq", "chip"),
            P("seq", "chip"),
            image,
            image,
            image,
        ),
        out_specs=image,
        check_vma=False,
    )
```

```python
import math

import jax
import jax.numpy as jnp
from jax import lax
from jax.experimental import pallas as pl
from jax.experimental.pallas import tpu as pltpu
from jax.sharding import PartitionSpec as P

D = 3072
HEAD_DIM = 128
CAP = 4
BLOCK = 16
NX = 4
NY = 4
NZ = 2
REPS = 8
PLANE = NX * NY
GROUP = PLANE * NZ
ROLES = 3
WIDE = ROLES * HEAD_DIM
IMG_DEV = 56
IMG = GROUP * IMG_DEV
SLOTS_PER_STEP = 8
STEP = SLOTS_PER_STEP * IMG_DEV
LANES = 896
SLOTS_A_STEP = LANES // IMG_DEV
ROWS = 256
SLOTS = ROWS // BLOCK * CAP
TEXT = REPS * SLOTS
FACTOR = math.log2(math.e) / math.sqrt(HEAD_DIM)
LOWEST = -1e30
VMEM_LIMIT = 60 * 1024 * 1024
MESH = pl.DeviceIdType.MESH

S_TEXT, S_MOD, S_STAT, S_REQ = 0, 1, 2, 3
S_W, S_WC, S_SUM, S_REP = 4, 6, 8, 10
S_OUT, S_HOP, S_LAST = 12, 13, 16
S_ALL = 28


def kernel(
    text, mod, step, req, w_key, w_value, q_in, k_in, v_in, out,
    tx, mod_v, md, rq, w, relay, final, stats, xs, acc, sum_s, sum_r,
    place_t, rep_s, landed, qh, kh, vh, m, l, o, o_s,
    ssem, rsem, lsem,
):
    f32, bf16 = jnp.float32, jnp.bfloat16
    rep, seq, z = lax.axis_index("rep"), lax.axis_index("seq"), lax.axis_index("chip")
    y, x = lax.div(seq, NX), lax.rem(seq, NX)
    role = lax.rem(x + y, NX)
    active = role < ROLES
    idle = role >= ROLES

    def group_at(px, py, pz):
        return (rep, py * NX + px, pz)

    def offsets(i):
        return lax.rem(i, NX), lax.div(i, SLOTS_PER_STEP), lax.rem(lax.div(i, NX), NZ)

    def ahead(i):
        dx, dy, dz = offsets(i)
        return lax.rem(x + dx, NX), lax.rem(y + dy, NY), lax.rem(z + dz, NZ)

    def behind(i):
        dx, dy, dz = offsets(i)
        return lax.rem(x + NX - dx, NX), lax.rem(y + NY - dy, NY), lax.rem(z + NZ - dz, NZ)

    def x_peer(d):
        return (rep, y * NX + lax.rem(x + d, NX), z)

    def y_peer(d):
        return (rep, lax.rem(y + d, NY) * NX + x, z)

    def rep_peer(d):
        return (lax.rem(rep + d, REPS), seq, z)

    def head_columns(head):
        return pl.ds(pl.multiple_of(head * HEAD_DIM, HEAD_DIM), HEAD_DIM)

    def columns(index):
        return pl.ds(pl.multiple_of(index * WIDE, WIDE), WIDE)

    own_head = head_columns((z * NY + y) * ROLES + role)

    def remote(src, dst, index, peer):
        return pltpu.make_async_remote_copy(
            src_ref=src, dst_ref=dst, send_sem=ssem.at[index], recv_sem=rsem.at[index],
            device_id=peer, device_id_type=MESH,
        )

    def send(src, dst, index, peer):
        remote(src, dst, index, peer).start()

    def arrived(ref, index):
        remote(ref, ref, index, x_peer(1)).wait_recv()

    def left(ref, index):
        remote(ref, ref, index, x_peer(1)).wait_send()

    barrier = pltpu.get_barrier_semaphore()

    def greet(i, carry):
        pl.semaphore_signal(barrier, inc=1, device_id=group_at(*ahead(i)), device_id_type=MESH)
        return carry

    lax.fori_loop(1, GROUP, greet, 0)
    for d in range(1, REPS):
        pl.semaphore_signal(barrier, inc=1, device_id=rep_peer(d), device_id_type=MESH)

    own = [
        pltpu.make_async_copy(text, tx.at[0], lsem.at[0]),
        pltpu.make_async_copy(mod, mod_v, lsem.at[1]),
        pltpu.make_async_copy(req, rq.at[rep], lsem.at[2]),
    ]
    own_text, own_mod, own_req = own
    for copy in own:
        copy.start()

    core = lax.rem(rep, 2)
    sibling = (rep + 1 - 2 * core, seq, z)
    both = rep - core

    def on_core(number, src, what):
        @pl.when(core == number)
        def _():
            what(src)

    def own_weights(src):
        return pltpu.make_async_copy(src.at[:, columns(y)], w.at[0], lsem.at[3])

    on_core(0, w_key, lambda src: own_weights(src).start())
    on_core(1, w_value, lambda src: own_weights(src).start())

    def role_at(px, py):
        return lax.rem(px + py, NX)

    def head_at(px, py, pz):
        return head_columns((pz * NY + py) * ROLES + role_at(px, py))

    image = (q_in, k_in, v_in)

    def own_hop(t, d):
        py = lax.rem(y + d, NY)
        return pltpu.make_async_copy(
            image[t].at[0, :, head_at(x, py, z)], relay.at[t, d, 0], lsem.at[5 + NY * t + d]
        )

    for d in range(NY):

        @pl.when(role_at(x, y + d) < ROLES)
        def _(d=d):
            for t in range(3):
                own_hop(t, d).start()

    pl.semaphore_wait(barrier, GROUP - 1 + REPS - 1)

    for d in range(1, NY):
        send(text, tx.at[d], S_TEXT, y_peer(d))

    own_mod.wait()
    for g in range(REPS):
        md[0, 2 * g : 2 * g + 2, :] = mod_v[step[g]]
    for d in range(1, NY):
        send(md.at[0], md.at[d], S_MOD, y_peer(d))

    own_text.wait()
    part = tx[0].astype(f32)
    stats[0] = jnp.concatenate(
        [
            jnp.sum(part, axis=0, keepdims=True),
            jnp.sum(part * part, axis=0, keepdims=True),
            jnp.zeros((6, ROWS), f32),
        ],
        axis=0,
    )

    def send_stats(i, carry):
        px, py = lax.rem(x + lax.rem(i, NX), NX), lax.rem(y + lax.div(i, NX), NY)
        send(stats.at[0], stats.at[i], S_STAT, group_at(px, py, z))
        return carry

    lax.fori_loop(1, PLANE, send_stats, 0)

    for d in range(1, REPS):
        send(req, rq.at[rep], S_REQ, rep_peer(d))

    def send_weights(src):
        for d in range(1, NY):
            send(src.at[:, columns(lax.rem(y + d, NY))], w.at[d], S_W, y_peer(d))

    on_core(0, w_key, send_weights)
    on_core(1, w_value, send_weights)

    for t in range(3):

        def first_hop(n, carry, t=t):
            i = lax.rem(n, SLOTS_PER_STEP - 1) + 1
            d = lax.div(n, SLOTS_PER_STEP - 1)
            px, _, pz = ahead(i)
            py = lax.rem(y + d, NY)

            @pl.when(role_at(px, py) < ROLES)
            def _():
                send(image[t].at[0, :, head_at(px, py, pz)], relay.at[t, d, i], S_HOP + t, group_at(px, y, pz))

            return carry

        lax.fori_loop(0, NY * (SLOTS_PER_STEP - 1), first_hop, 0)

    own_req.wait()
    request = rq[rep]
    sub16 = lax.broadcasted_iota(jnp.int32, (16, ROWS), 0)
    pick_shift = (sub16 == 2 * request).astype(f32)
    pick_scale = (sub16 == 2 * request + 1).astype(f32)

    def second_hop(t):
        arrived(relay.at[t, 0:ROLES, 1:SLOTS_PER_STEP], S_HOP + t)
        for d in (1, 3, 2, 0):

            @pl.when(role_at(x, y + d) < ROLES)
            def _(d=d):
                own_hop(t, d).wait()
                if d > 0:
                    send(relay.at[t, d], final.at[t, d], S_LAST + NY * t + d, y_peer(d))

    arrived(md.at[1:NY], S_MOD)
    arrived(stats.at[1:PLANE], S_STAT)
    summed = stats[0]
    for i in range(1, PLANE):
        summed = summed + stats[i]
    mean = summed[0:1] / D
    power = summed[1:2] / D
    scaled = lax.rsqrt(power - mean * mean + 1e-06)
    over_rows = (((0,), (0,)), ((), ()))
    arrived(tx.at[1:NY], S_TEXT)
    for d in range(NY):
        shift = lax.dot_general(
            md[d], pick_shift, over_rows, precision=lax.Precision.HIGHEST, preferred_element_type=f32
        )
        scale = lax.dot_general(
            md[d], pick_scale, over_rows, precision=lax.Precision.HIGHEST, preferred_element_type=f32
        )
        shaped = (tx[d].astype(f32) - mean) * scaled * (1.0 + scale) + shift
        xs[core, d] = shaped.astype(bf16)
    send(xs.at[core], xs.at[core], S_WC, sibling)

    second_hop(0)
    arrived(w.at[1:NY], S_W)
    on_core(0, w_key, lambda src: own_weights(src).wait())
    on_core(1, w_value, lambda src: own_weights(src).wait())
    arrived(xs.at[0], S_WC)
    for part in range(2):
        acc[part] = lax.dot_general(
            xs[part].reshape(D // NX, ROWS), w[...].reshape(D // NX, WIDE), over_rows,
            preferred_element_type=f32,
        )
        sum_s[part] = acc[part].astype(bf16)
        for d in range(1, NX):
            its_role = lax.rem(x + d + y, NX)

            @pl.when(its_role < ROLES)
            def _(part=part, d=d, its_role=its_role):
                src = sum_s.at[part, :, head_columns(its_role)]
                send(src, sum_r.at[part, d], S_SUM + part, x_peer(d))

    second_hop(1)
    second_hop(2)

    arrived(rq.at[1:REPS], S_REQ)
    first_row = lax.broadcasted_iota(jnp.int32, (ROWS, ROWS), 0)
    second_row = lax.broadcasted_iota(jnp.int32, (ROWS, ROWS), 1)
    earlier = (first_row < second_row).astype(f32).astype(bf16)
    for part in range(2):
        request = rq[both + part]
        is_target = sub16 == request
        count = jnp.dot(is_target.astype(f32).astype(bf16), earlier, preferred_element_type=f32)
        slot = jnp.sum(jnp.where(is_target, count, 0.0), axis=0, keepdims=True).astype(jnp.int32)
        is_place = lax.broadcasted_iota(jnp.int32, (TEXT, ROWS), 0) == request * SLOTS + slot
        place_t[part] = is_place.astype(f32).astype(bf16)

    @pl.when(active)
    def _():
        over_columns = (((1,), (1,)), ((), ()))

        def flatten(block):
            return block.astype(f32).reshape(STEP, HEAD_DIM).astype(bf16)

        def update(lanes, s, values, first):
            newest = jnp.max(s, axis=0, keepdims=True)
            if not first:
                newest = jnp.maximum(m[:, lanes], newest)
            weights = jnp.exp2((s - newest) * FACTOR)
            total = jnp.sum(weights, axis=0, keepdims=True)
            mixed = lax.dot_general(values, weights.astype(bf16), over_rows, preferred_element_type=f32)
            if not first:
                fade = jnp.exp2((m[:, lanes] - newest) * FACTOR)
                total = l[:, lanes] * fade + total
                mixed = o[:, lanes] * fade + mixed
            m[:, lanes] = newest
            l[:, lanes] = total
            o[:, lanes] = mixed

        def image_chunk(c):
            for t, dst in ((1, kh), (2, vh)):
                if c > 0:
                    arrived(final.at[t, c], S_LAST + NY * t + c)
                dst[...] = flatten((final if c > 0 else relay)[t, c])

            def image_step(b, carry):
                lanes = pl.ds(pl.multiple_of(b * LANES, LANES), LANES)
                s = lax.dot_general(kh[...], qh[lanes, :], over_columns, preferred_element_type=f32)
                update(lanes, s, vh[...], c == 0)
                return carry

            lax.fori_loop(0, IMG // LANES, image_step, 0)

        for d in (0, 1, 3, 2):
            if d > 0:
                arrived(final.at[0, d], S_LAST + d)
            qh[pl.ds(d * STEP, STEP), :] = flatten((final if d > 0 else relay)[0, d])

        for part in range(2):
            arrived(sum_r.at[part, 1:NX], S_SUM + part)
            rows = acc[part, :, head_columns(role)]
            for d in range(1, NX):
                rows = rows + sum_r[part, d].astype(f32)
            moved = jnp.dot(place_t[part], rows.astype(bf16), preferred_element_type=f32)
            rep_s[part] = moved.astype(bf16).reshape(REPS, SLOTS, HEAD_DIM)
            for d in range(1, REPS):
                src = rep_s.at[part, lax.rem(rep + d, REPS)]
                send(src, landed.at[core, both + part], S_REP, rep_peer(d))
            landed[core, both + part] = rep_s[part, rep]

        image_chunk(0)
        image_chunk(3)
        image_chunk(1)
        image_chunk(2)


        named = jnp.concatenate([rq[d] for d in range(REPS)], axis=0) == rep
        counted = jnp.sum(jnp.where(named, 1.0, 0.0), axis=1, keepdims=True)
        slot_number = lax.broadcasted_iota(jnp.int32, (SLOTS, HEAD_DIM), 0).astype(f32)
        live = jnp.concatenate([slot_number < counted[d : d + 1] for d in range(REPS)], axis=0)

        arrived(landed.at[0:2, 1:REPS], S_REP)

        def text_step(n, carry):
            b = IMG // LANES - 1 - n
            lanes = pl.ds(pl.multiple_of(b * LANES, LANES), LANES)
            keys = landed[0].reshape(TEXT, HEAD_DIM)
            values = landed[1].reshape(TEXT, HEAD_DIM)
            s = lax.dot_general(keys, qh[lanes, :], over_columns, preferred_element_type=f32)
            update(lanes, jnp.where(live[:, 0:1], s, LOWEST), values, False)
            result = (o[:, lanes] / l[:, lanes]).T.reshape(SLOTS_A_STEP, IMG_DEV, HEAD_DIM)
            o_s[pl.ds(b * SLOTS_A_STEP, SLOTS_A_STEP)] = result.astype(bf16)

            def send_result(k, inner):
                i = b * SLOTS_A_STEP + SLOTS_A_STEP - 1 - k

                @pl.when(i > 0)
                def _():
                    send(o_s.at[i], out.at[0, :, own_head], S_OUT, group_at(*behind(i)))

                return inner

            lax.fori_loop(0, SLOTS_A_STEP, send_result, 0)
            return carry

        lax.fori_loop(0, IMG // LANES, text_step, 0)
        last = pltpu.make_async_copy(o_s.at[0], out.at[0, :, own_head], lsem.at[17])
        last.start()
        arrived(out.at[0, :, 0 : (NY * NZ * ROLES - 1) * HEAD_DIM], S_OUT)
        last.wait()
        left(o_s.at[1:GROUP], S_OUT)
        for part in range(2):
            left(sum_r.at[part, 1 : NX - 1], S_SUM + part)
        left(landed.at[0:2, 1:REPS], S_REP)

    @pl.when(idle)
    def _():
        arrived(out.at[0], S_OUT)
        for part in range(2):
            left(sum_r.at[part, 1:NX], S_SUM + part)

    for t in range(3):
        left(relay.at[t, 0:ROLES, 1:SLOTS_PER_STEP], S_HOP + t)
        for d in range(1, NY):

            @pl.when(role_at(x, y + d) < ROLES)
            def _(t=t, d=d):
                left(relay.at[t, d], S_LAST + NY * t + d)

    left(tx.at[1:NY], S_TEXT)
    left(md.at[1:NY], S_MOD)
    left(stats.at[1:PLANE], S_STAT)
    left(rq.at[1:REPS], S_REQ)
    left(w.at[1:NY], S_W)
    left(xs.at[0], S_WC)


def local(text_rows, modulation, timestep, row_request, w_key, w_value, q_image, k_image, v_image):
    f32, bf16 = jnp.float32, jnp.bfloat16
    smem = pl.BlockSpec(memory_space=pltpu.SMEM)
    hbm = pl.BlockSpec(memory_space=pl.ANY)
    features = text_rows.shape[1]
    blocks = pltpu.VMEM((GROUP, IMG_DEV, HEAD_DIM), bf16)
    hops = pltpu.VMEM((3, NY, SLOTS_PER_STEP, IMG_DEV, HEAD_DIM), bf16)
    return pl.pallas_call(
        kernel,
        out_shape=jax.ShapeDtypeStruct(q_image.shape, bf16),
        in_specs=[hbm, hbm, smem, hbm, hbm, hbm, hbm, hbm, hbm],
        out_specs=hbm,
        scratch_shapes=[
            pltpu.VMEM((NY, features, ROWS), bf16),
            pltpu.VMEM(modulation.shape, f32),
            pltpu.VMEM((NY, 2 * REPS, features), f32),
            pltpu.VMEM((REPS, 1, ROWS), jnp.int32),
            pltpu.VMEM((NY, features, WIDE), bf16),
            hops,
            hops,
            pltpu.VMEM((PLANE, 8, ROWS), f32),
            pltpu.VMEM((2, NY, features, ROWS), bf16),
            pltpu.VMEM((2, ROWS, WIDE), f32),
            pltpu.VMEM((2, ROWS, WIDE), bf16),
            pltpu.VMEM((2, NX, ROWS, HEAD_DIM), bf16),
            pltpu.VMEM((2, TEXT, ROWS), bf16),
            pltpu.VMEM((2, REPS, SLOTS, HEAD_DIM), bf16),
            pltpu.VMEM((2, REPS, SLOTS, HEAD_DIM), bf16),
            pltpu.VMEM((IMG, HEAD_DIM), bf16),
            pltpu.VMEM((STEP, HEAD_DIM), bf16),
            pltpu.VMEM((STEP, HEAD_DIM), bf16),
            pltpu.VMEM((1, IMG), f32),
            pltpu.VMEM((1, IMG), f32),
            pltpu.VMEM((HEAD_DIM, IMG), f32),
            blocks,
            pltpu.SemaphoreType.DMA((S_ALL,)),
            pltpu.SemaphoreType.DMA((S_ALL,)),
            pltpu.SemaphoreType.DMA((18,)),
        ],
        compiler_params=pltpu.CompilerParams(
            collective_id=0, has_side_effects=True, vmem_limit_bytes=VMEM_LIMIT
        ),
    )(
        text_rows.T, modulation, timestep, row_request.reshape(1, -1),
        w_key, w_value, q_image, k_image, v_image,
    )


def solution(mesh):
    image = P("rep", ("seq", "chip"), None)
    return jax.shard_map(
        local,
        mesh=mesh,
        in_specs=(
            P("rep", "seq"),
            P(None, None, "seq"),
            P(),
            P("rep", None),
            P("seq", "chip"),
            P("seq", "chip"),
            image,
            image,
            image,
        ),
        out_specs=image,
        check_vma=False,
    )
```
